256 devices in a mesh: row: 16 (over z_hi, x, core), col: 16 (over z_lo, y).
Axes of the slice: x: 4, y: 4, z: 8 (z_hi: 2, z_lo: 4; z = z_hi * 4 + z_lo), core: 2. Of those that a mesh axis runs over, the one named last changes fastest.
Arguments:
- matrix: float32 [16384, 16384], P('row', 'col'), as said below
Outputs:
- updated: float32 [16384, 16384], P('row', 'col')
- r_factor: float32 [256, 256], replicated
Inputs may be any that keep to these rules, and one draw needn't show every extreme that they name: matrix is symmetric once read in global order; its entries are of order one, those of a symmetric normal matrix, possibly plus a small symmetric rank-one term, scaled on both sides by row factors between 0.3 and 3.
All inputs are finite; a program needn't handle non-finite values.
Results may differ from the reference program's by a relative error of at most 0.00013.
Values sent between devices are 32-bit elements; how exact they have to be, the bound alone decides.
A program may use at most 128 MiB of HBM per device.

```python
import math
import jax
import jax.numpy as jnp
from jax import lax

NB = 256
MATRIX = 16384
GRID_ROWS = 16
GRID_COLS = 16
ROW_BLOCKS = 4
COL_BLOCKS = 4


def draw_matrix(key, part):
    key = jax.random.fold_in(key, 11)
    first, second = jax.random.split(key, 2)
    base = jax.random.normal(first, (MATRIX, MATRIX), jnp.float32)
    sym = (base + base.T) * 0.70710678
    scales = jnp.exp(jax.random.uniform(second, (MATRIX,), jnp.float32, math.log(0.4), math.log(2.5)))
    whole = scales[:, None] * sym * scales[None, :]
    stored = whole.reshape(ROW_BLOCKS, GRID_ROWS, NB, COL_BLOCKS, GRID_COLS, NB)
    return stored.transpose(1, 0, 2, 4, 3, 5).reshape(MATRIX, MATRIX)


def setup_inputs(seed: int = 0) -> dict:
    keys = jax.random.split(jax.random.key(seed), 2)
    matrix = draw_matrix(jax.random.fold_in(keys[1], 71), 0)
    return {"matrix": matrix}


def row_storage(values):
    breadth = values.shape[1]
    return values.reshape(ROW_BLOCKS, GRID_ROWS, NB, breadth).transpose(1, 0, 2, 3).reshape(MATRIX, breadth)

def row_global(values):
    breadth = values.shape[1]
    return values.reshape(GRID_ROWS, ROW_BLOCKS, NB, breadth).transpose(1, 0, 2, 3).reshape(MATRIX, breadth)

def col_storage(values):
    breadth = values.shape[1]
    return values.reshape(COL_BLOCKS, GRID_COLS, NB, breadth).transpose(1, 0, 2, 3).reshape(MATRIX, breadth)

def product(left, right):
    return jnp.dot(left.astype(jnp.float32), right.astype(jnp.float32), precision=lax.Precision.HIGHEST, preferred_element_type=jnp.float32)

def reference(matrix):
    panel = row_global(matrix[:, :NB])
    keep = jnp.arange(MATRIX, dtype=jnp.int32) >= NB
    panel = jnp.where(keep[:, None], panel, jnp.float32(0.0))
    gram = product(panel.T, panel)
    lower = jnp.linalg.cholesky(gram)
    basis = lax.linalg.triangular_solve(lower, panel, left_side=False, lower=True, transpose_a=True)
    q_rows = row_storage(basis)
    q_cols = col_storage(basis)
    image_rows = product(matrix, q_cols)
    curvature = product(q_rows.T, image_rows)
    sweep_rows = 2.0 * image_rows - 2.0 * product(q_rows, curvature)
    sweep_cols = col_storage(row_global(sweep_rows))
    updated = matrix - product(q_rows, sweep_cols.T) - product(sweep_rows, q_cols.T)
    return (updated, lower.T)
```

```python
import functools
import jax
import jax.numpy as jnp
from jax import lax
from jax.experimental import pallas as pl
from jax.experimental.pallas import tpu as pltpu
from jax.sharding import PartitionSpec as P

NB = 256
N = 1024
CH = 16
MESH = pl.DeviceIdType.MESH
F32 = jnp.float32
BF16 = jnp.bfloat16

LAST = (((1,), (1,)), ((), ()))
FIRST = (((0,), (0,)), ((), ()))
PLAIN = (((1,), (0,)), ((), ()))


def split(x):
    hi = x.astype(BF16)
    lo = (x - hi.astype(F32)).astype(BF16)
    return hi, lo


def dot(a, b, dims):
    return lax.dot_general(a, b, dims, preferred_element_type=F32)


def dot3s(a, b, dims):
    (ah, al), (bh, bl) = a, b
    return dot(ah, bh, dims) + (dot(ah, bl, dims) + dot(al, bh, dims))


def dot3(a, b, dims):
    return dot3s(split(a), split(b), dims)


def dot6(a, b, dims):
    return lax.dot_general(a, b, dims, precision=lax.Precision.HIGHEST, preferred_element_type=F32)


def chunk(k):
    return pl.ds(pl.multiple_of(k * CH, CH), CH)


class Sends:
    def __init__(self, sems):
        self.sems = sems
        self.count = 0
        self.pending = []

    def go(self, src, dst, recv, dev, cond=None):
        copy = pltpu.make_async_remote_copy(
            src_ref=src, dst_ref=dst, send_sem=self.sems.at[self.count], recv_sem=recv, device_id=dev, device_id_type=MESH
        )
        self.count += 1
        self.pending.append((copy, cond))
        when(cond, copy.start)

    def drain(self):
        for copy, cond in self.pending:
            when(cond, copy.wait_send)
        self.pending = []


def when(cond, fn):
    if cond is None:
        fn()
    else:
        pl.when(cond)(fn)


def arrived(ref, recv, send, cond=None):
    copy = pltpu.make_async_copy(ref, ref, recv)
    when(cond, copy.wait)


def exchange_kernel(
    s_hbm, pr, pc, wr, wc, gf, cf,
    s, wp, r1, t, r2, u, r3, gp, grs, crs,
    load_sem, send_sem, gsend, gasend, csend, casend,
    pr_sem, pc_sem, wr_sem, wc_sem, r1_sem, r2_sem, r3_sem, grs_sem, gf_sem, crs_sem, cf_sem,
):
    p = lax.axis_index("row")
    q = lax.axis_index("col")
    zh, x, c = p // 8, (p // 2) % 4, p % 2
    zl, y = q // 4, q % 4

    load = pltpu.make_async_copy(s_hbm, s, load_sem)
    load.start()

    def row_of(zh_, x_, c_):
        return zh_ * 8 + x_ * 2 + c_

    barrier = pltpu.get_barrier_semaphore()

    def greet(i, carry):
        pl.semaphore_signal(barrier, inc=1, device_id=(lax.rem(p + i, 16), q), device_id_type=MESH)
        pl.semaphore_signal(barrier, inc=1, device_id=(p, lax.rem(q + i, 16)), device_id_type=MESH)
        return carry

    lax.fori_loop(1, 16, greet, 0)

    @pl.when(p != q)
    def _():
        pl.semaphore_signal(barrier, inc=1, device_id=(q, p), device_id_type=MESH)
        pl.semaphore_wait(barrier, 31)

    @pl.when(p == q)
    def _():
        pl.semaphore_wait(barrier, 30)

    load.wait()
    out = Sends(send_sem)


    def col_start(buf, sems, root):
        for i in (1, 2, 3):
            d = lax.rem(zl + i, 4) * 4 + y
            out.go(buf.at[chunk(q)], buf.at[chunk(q)], sems.at[q], (p, d), (d != 0) if root else None)
        for i in (1, 3, 2):
            d = zl * 4 + lax.rem(y + i, 4)
            out.go(buf.at[chunk(q)], buf.at[chunk(q)], sems.at[q], (p, d), (d != 0) if root else None)

    def col_forward(buf, sems, root):
        for i in (1, 3, 2):
            k = lax.rem(zl + i, 4) * 4 + y
            arrived(buf.at[chunk(k)], sems.at[k], None, (q != 0) if root else None)
            for j in (1, 3, 2):
                d = zl * 4 + lax.rem(y + j, 4)
                out.go(buf.at[chunk(k)], buf.at[chunk(k)], sems.at[k], (p, d), (d != 0) if root else None)

    def col_finish(buf, sems, root):
        for i in (0, 1, 3, 2):
            for j in (1, 3, 2):
                k = lax.rem(zl + i, 4) * 4 + lax.rem(y + j, 4)
                arrived(buf.at[chunk(k)], sems.at[k], None, (q != 0) if root else None)

    def row_send(buf, sems, k, d, root):
        out.go(buf.at[chunk(k)], buf.at[chunk(k)], sems.at[k], (d, q), (d != 0) if root else None)

    def row_start(buf, sems, root):
        row_send(buf, sems, p, row_of(1 - zh, x, c), root)
        for i in (1, 3, 2):
            row_send(buf, sems, p, row_of(zh, lax.rem(x + i, 4), c), root)
        row_send(buf, sems, p, row_of(zh, x, 1 - c), root)

    def row_partner(buf, sems, root):
        k = row_of(1 - zh, x, c)
        arrived(buf.at[chunk(k)], sems.at[k], None, (p != 0) if root else None)
        for i in (1, 3, 2):
            row_send(buf, sems, k, row_of(zh, lax.rem(x + i, 4), c), root)
        row_send(buf, sems, k, row_of(zh, x, 1 - c), root)

    def row_own(buf, sems, root, z):
        for i in (1, 3, 2):
            k = row_of(z, lax.rem(x + i, 4), c)
            arrived(buf.at[chunk(k)], sems.at[k], None, (p != 0) if root else None)
            row_send(buf, sems, k, row_of(zh, x, 1 - c), root)

    def row_finish(buf, sems, root):
        for z in (zh, 1 - zh):
            for i in (0, 1, 3, 2):
                k = row_of(z, lax.rem(x + i, 4), 1 - c)
                arrived(buf.at[chunk(k)], sems.at[k], None, (p != 0) if root else None)

    lane = lax.broadcasted_iota(jnp.int32, (NB, N), 1)

    @pl.when(p == 0)
    def _():
        pc[...] = jnp.where((q == 0) & (lane < NB), 0.0, s[0:NB, :])

    for k in (14, 15, 12, 13, 10, 11, 8, 9, 6, 7, 4, 5, 2, 3, 1):
        out.go(pc.at[chunk(k)], pc.at[chunk(k)], pc_sem.at[k], (k, q), p == 0)

    @pl.when(q == 0)
    def _():
        pr[...] = jnp.where((p == 0) & (lane < NB), 0.0, s[:, 0:NB].T)

    for k in (15, 14, 13, 12, 11, 10, 9, 8, 7, 6, 5, 4, 3, 2, 1):
        out.go(pr.at[chunk(k)], pr.at[chunk(k)], pr_sem.at[k], (p, k), q == 0)

    arrived(pr.at[chunk(q)], pr_sem.at[q], None, q != 0)
    col_start(pr, pr_sem, True)
    arrived(pc.at[chunk(p)], pc_sem.at[p], None, p != 0)
    row_start(pc, pc_sem, True)
    col_forward(pr, pr_sem, True)
    row_partner(pc, pc_sem, True)
    row_own(pc, pc_sem, True, zh)
    row_own(pc, pc_sem, True, 1 - zh)
    row_finish(pc, pc_sem, True)

    gp[...] = dot3(pc[...], pc[...], LAST)
    grs[pl.ds(q, 1)] = gp[chunk(q), :][None]

    def direct(i, src, dst, ssem, rsem, dev):
        return pltpu.make_async_remote_copy(
            src_ref=src, dst_ref=dst, send_sem=ssem, recv_sem=rsem, device_id=dev, device_id_type=MESH
        )

    def gram_copy(i):
        d = lax.rem(q + i, 16)
        return direct(i, gp.at[chunk(d)], grs.at[q], gsend.at[i], grs_sem.at[q], (p, d))

    def gram_all(i):
        d = lax.rem(q + i, 16)
        return direct(i, gf.at[chunk(q)], gf.at[chunk(q)], gasend.at[i], gf_sem.at[q], (p, d))

    def curv_copy(i):
        d = lax.rem(q + i, 16)
        return direct(i, crs.at[q], crs.at[q], csend.at[i], crs_sem.at[q], (p, d))

    def curv_all(i):
        d = lax.rem(p + i, 16)
        return direct(i, cf.at[chunk(p)], cf.at[chunk(p)], casend.at[i], cf_sem.at[p], (d, q))

    def start_all(make):
        lax.fori_loop(1, 16, lambda i, z: (make(i).start(), z)[1], 0)

    def drain_all(make):
        lax.fori_loop(1, 16, lambda i, z: (make(i).wait_send(), z)[1], 0)

    def wait_slots(buf, sems, me):
        def step(i, z):
            k = lax.rem(me + i, 16)
            arrived(buf.at[k], sems.at[k], None)
            return z

        lax.fori_loop(1, 16, step, 0)

    def wait_chunks(buf, sems, me):
        def step(i, z):
            k = lax.rem(me + i, 16)
            arrived(buf.at[chunk(k)], sems.at[k], None)
            return z

        lax.fori_loop(1, 16, step, 0)

    start_all(gram_copy)
    col_finish(pr, pr_sem, True)

    ph, plo = split(pr[...])
    wp4 = wp.reshape(NB, N)

    def product(j, z):
        cols = pl.ds(pl.multiple_of(j * 256, 256), 256)
        wp4[:, cols] = dot3s((ph, plo), split(s[:, cols]), PLAIN)
        return z

    lax.fori_loop(0, 4, product, 0)

    out.go(wp.at[:, 1 - c], r1, r1_sem, (row_of(zh, x, 1 - c), q))

    wait_slots(grs, grs_sem, q)
    gf[chunk(q), :] = jnp.sum(grs[...], axis=0)
    start_all(gram_all)

    arrived(r1, r1_sem, None)
    t[...] = wp[:, pl.ds(c, 1)][:, 0] + r1[...]
    for phase, z in ((0, 1 - zh), (1, zh)):
        for i in (1, 3, 2):
            xx = lax.rem(x + i, 4)
            out.go(t.at[z * 4 + xx], r2.at[phase, i - 1], r2_sem.at[phase, i - 1], (row_of(zh, xx, c), q))
    for i in (1, 3, 2):
        arrived(r2.at[0, i - 1], r2_sem.at[0, i - 1], None)
    u[...] = t[(1 - zh) * 4 + x] + (r2[0, 0] + r2[0, 1] + r2[0, 2])
    out.go(u, r3, r3_sem, (row_of(1 - zh, x, c), q))
    for i in (1, 3, 2):
        arrived(r2.at[1, i - 1], r2_sem.at[1, i - 1], None)
    part = t[zh * 4 + x] + (r2[1, 0] + r2[1, 1] + r2[1, 2])
    arrived(r3, r3_sem, None)
    mine = part + r3[...]
    wc[chunk(p), :] = mine

    out.go(wc.at[chunk(p)], wr.at[chunk(p)], wr_sem.at[p], (q, p), p != q)

    @pl.when(p == q)
    def _():
        wr[chunk(q), :] = mine

    row_start(wc, wc_sem, False)
    crs[pl.ds(q, 1)] = dot3(mine, pc[...], LAST)[None]
    start_all(curv_copy)
    arrived(wr.at[chunk(q)], wr_sem.at[q], None, p != q)
    col_start(wr, wr_sem, False)
    row_partner(wc, wc_sem, False)
    row_own(wc, wc_sem, False, zh)
    col_forward(wr, wr_sem, False)
    wait_slots(crs, crs_sem, q)
    cf[chunk(p), :] = jnp.sum(crs[...], axis=0)
    start_all(curv_all)
    row_own(wc, wc_sem, False, 1 - zh)
    row_finish(wc, wc_sem, False)
    wait_chunks(gf, gf_sem, q)
    wait_chunks(cf, cf_sem, p)
    col_finish(wr, wr_sem, False)
    out.drain()
    for make in (gram_copy, gram_all, curv_copy, curv_all):
        drain_all(make)


def exchange(matrix):
    vm = pl.BlockSpec(memory_space=pltpu.VMEM)
    dma = pltpu.SemaphoreType.DMA
    big = jax.ShapeDtypeStruct((NB, N), F32)
    small = jax.ShapeDtypeStruct((NB, NB), F32)
    return pl.pallas_call(
        exchange_kernel,
        out_shape=(big, big, big, big, small, small),
        in_specs=[pl.BlockSpec(memory_space=pl.ANY)],
        out_specs=(vm,) * 6,
        scratch_shapes=[
            pltpu.VMEM((N, N), F32),
            pltpu.VMEM((8, 2, CH, N), F32),
            pltpu.VMEM((8, CH, N), F32),
            pltpu.VMEM((8, CH, N), F32),
            pltpu.VMEM((2, 3, CH, N), F32),
            pltpu.VMEM((CH, N), F32),
            pltpu.VMEM((CH, N), F32),
            pltpu.VMEM((NB, NB), F32),
            pltpu.VMEM((16, CH, NB), F32),
            pltpu.VMEM((16, CH, NB), F32),
            dma, dma((128,)), dma((16,)), dma((16,)), dma((16,)), dma((16,)),
            dma((16,)), dma((16,)), dma((16,)), dma((16,)), dma, dma((2, 3)), dma, dma((16,)), dma((16,)), dma((16,)), dma((16,)),
        ],
        compiler_params=pltpu.CompilerParams(collective_id=0, has_side_effects=True, vmem_limit_bytes=40 << 20),
        name="exchange",
    )(matrix)


def factor(aug):
    b = 64
    row = lax.broadcasted_iota(jnp.int32, (b, 2 * b), 0)
    col = lax.broadcasted_iota(jnp.int32, (b, 2 * b), 1)
    eye = (row + b == col).astype(F32)
    for k in range(4):
        here = slice(k * b, (k + 1) * b)
        a = jnp.concatenate([aug[here, here], eye[:, b:]], axis=1)
        for j in range(0, b, 2):
            c0, c1 = a[:, j : j + 1], a[:, j + 1 : j + 2]
            r0, r1 = a[j : j + 1, :], a[j + 1 : j + 2, :]
            a00, a01, a11 = a[j : j + 1, j : j + 1], a[j : j + 1, j + 1 : j + 2], a[j + 1 : j + 2, j + 1 : j + 2]
            inv = 1.0 / (a00 * a11 - a01 * a01)
            w0 = (a11 * r0 - a01 * r1) * inv
            w1 = (a00 * r1 - a01 * r0) * inv
            rest = c0 * w0 + c1 * w1
            second = (a01 / a00) * r0
            a = a - jnp.where(row > j + 1, rest, jnp.where(row == j + 1, second, 0.0))
        diag = jnp.sum(jnp.where(row == col, a, 0.0), axis=1, keepdims=True)
        inverse = (a * lax.rsqrt(diag))[:, b:]
        done = dot6(inverse, aug[here, :], PLAIN)
        aug[here, :] = done
        if k < 3:
            below = slice((k + 1) * b, NB)
            aug[below, :] = aug[below, :] - dot6(done[:, 0:NB], done, FIRST)[below, :]


def finish_kernel(pr, pc, wr, wc, gf, cf, s, out, r, aug, left, right):
    @pl.when(pl.program_id(0) == 0)
    def _():
        row = lax.broadcasted_iota(jnp.int32, (NB, NB), 0)
        col = lax.broadcasted_iota(jnp.int32, (NB, NB), 1)
        aug[:, 0:NB] = gf[...]
        aug[:, NB:] = (row == col).astype(F32)
        factor(aug)
        r[...] = jnp.where(row <= col, aug[:, 0:NB], 0.0)
        inverse = aug[:, NB:]
        m = split(2.0 * dot6(inverse, inverse, FIRST))
        half = split(0.5 * cf[...])
        for panel, image, side in ((pr, wr, 0), (pc, wc, 1)):
            a = dot3s(m, split(panel[...]), PLAIN)
            v = image[...] - dot3s(half, split(a), PLAIN)
            if side == 0:
                ah, al = split(a.T)
                vh, vl = split(v.T)
                for i, block in enumerate((ah, vh, ah, vh, al, vl)):
                    left[:, i * NB : (i + 1) * NB] = block
            else:
                ah, al = split(a)
                vh, vl = split(v)
                for i, block in enumerate((vh, ah, vl, al, vh, ah)):
                    right[i * NB : (i + 1) * NB, :] = block

    rows = pl.ds(pl.multiple_of(pl.program_id(0) * TILE, TILE), TILE)
    out[...] = s[...] - dot(left[rows, :], right[...], PLAIN)


TILE = 128


def finish(parts, matrix):
    whole = lambda shape: pl.BlockSpec(shape, lambda i: (0, 0))
    big, small, tile = whole((NB, N)), whole((NB, NB)), pl.BlockSpec((TILE, N), lambda i: (i, 0))
    return pl.pallas_call(
        finish_kernel,
        grid=(N // TILE,),
        out_shape=(jax.ShapeDtypeStruct((N, N), F32), jax.ShapeDtypeStruct((NB, NB), F32)),
        in_specs=[big, big, big, big, small, small, tile],
        out_specs=(tile, small),
        scratch_shapes=[pltpu.VMEM((NB, 2 * NB), F32), pltpu.VMEM((N, 6 * NB), BF16), pltpu.VMEM((6 * NB, N), BF16)],
        compiler_params=pltpu.CompilerParams(vmem_limit_bytes=48 << 20),
        name="finish",
    )(*parts, matrix)


def on_device(matrix):
    return finish(exchange(matrix), matrix)


def solution(mesh):
    return jax.shard_map(
        on_device,
        mesh=mesh,
        in_specs=(P("row", "col"),),
        out_specs=(P("row", "col"), P()),
        check_vma=False,
    )
```

```python
import functools
import jax
import jax.numpy as jnp
from jax import lax
from jax.experimental import pallas as pl
from jax.experimental.pallas import tpu as pltpu
from jax.sharding import PartitionSpec as P

NB = 256
N = 1024
CH = 16
MESH = pl.DeviceIdType.MESH
F32 = jnp.float32
BF16 = jnp.bfloat16

LAST = (((1,), (1,)), ((), ()))
FIRST = (((0,), (0,)), ((), ()))
PLAIN = (((1,), (0,)), ((), ()))


def split(x):
    hi = x.astype(BF16)
    lo = (x - hi.astype(F32)).astype(BF16)
    return hi, lo


def dot(a, b, dims):
    return lax.dot_general(a, b, dims, preferred_element_type=F32)


def dot3s(a, b, dims):
    (ah, al), (bh, bl) = a, b
    return dot(ah, bh, dims) + (dot(ah, bl, dims) + dot(al, bh, dims))


def dot3(a, b, dims):
    return dot3s(split(a), split(b), dims)


def dot6(a, b, dims):
    return lax.dot_general(a, b, dims, precision=lax.Precision.HIGHEST, preferred_element_type=F32)


def chunk(k):
    return pl.ds(pl.multiple_of(k * CH, CH), CH)


class Sends:
    def __init__(self, sems):
        self.sems = sems
        self.count = 0
        self.pending = []

    def go(self, src, dst, recv, dev, cond=None):
        copy = pltpu.make_async_remote_copy(
            src_ref=src, dst_ref=dst, send_sem=self.sems.at[self.count], recv_sem=recv, device_id=dev, device_id_type=MESH
        )
        self.count += 1
        self.pending.append((copy, cond))
        when(cond, copy.start)

    def drain(self):
        for copy, cond in self.pending:
            when(cond, copy.wait_send)
        self.pending = []


def when(cond, fn):
    if cond is None:
        fn()
    else:
        pl.when(cond)(fn)


def arrived(ref, recv, send, cond=None):
    copy = pltpu.make_async_copy(ref, ref, recv)
    when(cond, copy.wait)


def reciprocal(x):
    y = pl.reciprocal(x, approx=True)
    return y * (2.0 - x * y)


def pivot8(step, a):
    tiles = [a[8 * t : 8 * t + 8, :] for t in range(8)]
    sub = lax.broadcasted_iota(jnp.int32, (8, 128), 0)
    full = lambda v: jnp.broadcast_to(v, (8, 128))
    cols = [[full(tile[:, i : i + 1]) for i in range(8)] for tile in tiles]
    e = [[full(cols[0][k][i : i + 1, :]) if k >= i else None for k in range(8)] for i in range(8)]
    rows = [full(tiles[0][i : i + 1, :]) for i in range(8)]
    scaled = []
    for i in range(8):
        inv = reciprocal(e[i][i])
        scaled.append(rows[i] * inv)
        for k in range(i + 1, 8):
            f = e[i][k] * inv
            rows[k] = rows[k] - f * rows[i]
            for n in range(k, 8):
                e[k][n] = e[k][n] - f * e[i][n]
            for t in range(1, 8):
                cols[t][k] = cols[t][k] - cols[t][i] * f
    top = rows[0]
    for i in range(1, 8):
        top = jnp.where(sub == i, rows[i], top)
    new = []
    for t in range(1, 8):
        term = cols[t][0] * scaled[0]
        for i in range(1, 8):
            term = term + cols[t][i] * scaled[i]
        new.append(tiles[t] - term * jnp.where(step + t < 8, 1.0, 0.0).astype(F32))
    return pltpu.roll(jnp.concatenate(new + [top], axis=0), 120, axis=1)


def factor_block(aug, k):
    b = 64
    row = lax.broadcasted_iota(jnp.int32, (b, 2 * b), 0)
    col = lax.broadcasted_iota(jnp.int32, (b, 2 * b), 1)
    here = slice(k * b, (k + 1) * b)
    eye = (row + b == col).astype(F32)
    a = jnp.concatenate([aug[here, here], eye[:, b:]], axis=1)
    a = lax.fori_loop(0, 8, pivot8, a)
    diag = jnp.sum(jnp.where(row + b == col, a, 0.0), axis=1, keepdims=True)
    inverse = (a * lax.rsqrt(diag))[:, :b]
    done = dot6(inverse, aug[here, :], PLAIN)
    aug[here, :] = done
    if k < 3:
        below = slice((k + 1) * b, NB)
        aug[below, :] = aug[below, :] - dot6(done[:, (k + 1) * b : NB], done, FIRST)


def exchange_kernel(
    s_hbm, left, right, rfac,
    pr, pc, wr, wc, gf, cf, s, wp, r1, t, r2, u, r3, gp, grs, crs, aug, ar, ac,
    load_sem, send_sem, gsend, gasend, csend, casend,
    pr_sem, pc_sem, wr_sem, wc_sem, r1_sem, r2_sem, r3_sem, grs_sem, gf_sem, crs_sem, cf_sem,
):
    p = lax.axis_index("row")
    q = lax.axis_index("col")
    zh, x, c = p // 8, (p // 2) % 4, p % 2
    zl, y = q // 4, q % 4

    load = pltpu.make_async_copy(s_hbm, s, load_sem)
    load.start()

    def row_of(zh_, x_, c_):
        return zh_ * 8 + x_ * 2 + c_

    barrier = pltpu.get_barrier_semaphore()

    def greet(i, carry):
        pl.semaphore_signal(barrier, inc=1, device_id=(lax.rem(p + i, 16), q), device_id_type=MESH)
        pl.semaphore_signal(barrier, inc=1, device_id=(p, lax.rem(q + i, 16)), device_id_type=MESH)
        return carry

    lax.fori_loop(1, 16, greet, 0)

    pl.semaphore_wait(barrier, 30)
    load.wait()
    out = Sends(send_sem)


    def col_start(buf, sems, root):
        for i in (1, 2, 3):
            d = lax.rem(zl + i, 4) * 4 + y
            out.go(buf.at[chunk(q)], buf.at[chunk(q)], sems.at[q], (p, d), (d != 0) if root else None)
        for i in (1, 3, 2):
            d = zl * 4 + lax.rem(y + i, 4)
            out.go(buf.at[chunk(q)], buf.at[chunk(q)], sems.at[q], (p, d), (d != 0) if root else None)

    def col_forward(buf, sems, root):
        for i in (1, 3, 2):
            k = lax.rem(zl + i, 4) * 4 + y
            arrived(buf.at[chunk(k)], sems.at[k], None, (q != 0) if root else None)
            for j in (1, 3, 2):
                d = zl * 4 + lax.rem(y + j, 4)
                out.go(buf.at[chunk(k)], buf.at[chunk(k)], sems.at[k], (p, d), (d != 0) if root else None)

    def col_finish(buf, sems, root):
        for i in (0, 1, 3, 2):
            for j in (1, 3, 2):
                k = lax.rem(zl + i, 4) * 4 + lax.rem(y + j, 4)
                arrived(buf.at[chunk(k)], sems.at[k], None, (q != 0) if root else None)

    def row_send(buf, sems, k, d, root):
        out.go(buf.at[chunk(k)], buf.at[chunk(k)], sems.at[k], (d, q), (d != 0) if root else None)

    def row_start(buf, sems, root):
        row_send(buf, sems, p, row_of(1 - zh, x, c), root)
        for i in (1, 3, 2):
            row_send(buf, sems, p, row_of(zh, lax.rem(x + i, 4), c), root)
        row_send(buf, sems, p, row_of(zh, x, 1 - c), root)

    def row_partner(buf, sems, root):
        k = row_of(1 - zh, x, c)
        arrived(buf.at[chunk(k)], sems.at[k], None, (p != 0) if root else None)
        for i in (1, 3, 2):
            row_send(buf, sems, k, row_of(zh, lax.rem(x + i, 4), c), root)
        row_send(buf, sems, k, row_of(zh, x, 1 - c), root)

    def row_own(buf, sems, root, z):
        for i in (1, 3, 2):
            k = row_of(z, lax.rem(x + i, 4), c)
            arrived(buf.at[chunk(k)], sems.at[k], None, (p != 0) if root else None)
            row_send(buf, sems, k, row_of(zh, x, 1 - c), root)

    def row_finish(buf, sems, root):
        for z in (zh, 1 - zh):
            for i in (0, 1, 3, 2):
                k = row_of(z, lax.rem(x + i, 4), 1 - c)
                arrived(buf.at[chunk(k)], sems.at[k], None, (p != 0) if root else None)

    pairs = pc.reshape(2, 8, CH, N)
    j = x * 2 + c
    no_root = p != 0

    def pair_send(k, d, cond):
        out.go(pairs.at[:, k], pairs.at[:, k], pc_sem.at[k], (d, q), cond)

    def pair_wait(k):
        arrived(pairs.at[:, k], pc_sem.at[k], None, no_root)

    lane = lax.broadcasted_iota(jnp.int32, (NB, N), 1)

    @pl.when(p == 0)
    def _():
        pc[...] = jnp.where((q == 0) & (lane < NB), 0.0, s[0:NB, :])

    for k in (4, 5, 2, 3, 6, 7, 1):
        pair_send(k, k, p == 0)

    @pl.when(q == 0)
    def _():
        pr[...] = jnp.where((p == 0) & (lane < NB), 0.0, s[:, 0:NB].T)

    for k in (15, 14, 13, 12, 11, 10, 9, 8, 7, 6, 5, 4, 3, 2, 1):
        out.go(pr.at[chunk(k)], pr.at[chunk(k)], pr_sem.at[k], (p, k), q == 0)

    near, far = zh == 0, zh == 1
    pl.when(near & no_root)(lambda: arrived(pairs.at[:, j], pc_sem.at[j], None))
    pair_send(j, row_of(1, x, c), near)

    def pair_spread(here):
        for i in (1, 3, 2):
            d = row_of(zh, lax.rem(x + i, 4), c)
            pair_send(j, d, here & (d != 0))
        d = row_of(zh, x, 1 - c)
        pair_send(j, d, here & (d != 0))

    pair_spread(near)
    arrived(pr.at[chunk(q)], pr_sem.at[q], None, q != 0)
    col_start(pr, pr_sem, True)
    pl.when(far)(lambda: arrived(pairs.at[:, j], pc_sem.at[j], None))
    pair_spread(far)
    col_forward(pr, pr_sem, True)
    for i in (1, 3, 2):
        k = lax.rem(x + i, 4) * 2 + c
        pair_wait(k)
        d = row_of(zh, x, 1 - c)
        pair_send(k, d, d != 0)
    for i in (0, 1, 3, 2):
        pair_wait(lax.rem(x + i, 4) * 2 + 1 - c)

    gp[...] = dot3(pc[...], pc[...], LAST)
    grs[pl.ds(q, 1)] = gp[chunk(q), :][None]

    def direct(i, src, dst, ssem, rsem, dev):
        return pltpu.make_async_remote_copy(
            src_ref=src, dst_ref=dst, send_sem=ssem, recv_sem=rsem, device_id=dev, device_id_type=MESH
        )

    def gram_copy(i):
        d = lax.rem(q + i, 16)
        return direct(i, gp.at[chunk(d)], grs.at[q], gsend.at[i], grs_sem.at[q], (p, d))

    def gram_all(i):
        d = lax.rem(q + i, 16)
        return direct(i, gf.at[chunk(q)], gf.at[chunk(q)], gasend.at[i], gf_sem.at[q], (p, d))

    def curv_copy(i):
        d = lax.rem(q + i, 16)
        return direct(i, crs.at[q], crs.at[q], csend.at[i], crs_sem.at[q], (p, d))

    def curv_all(i):
        d = lax.rem(p + i, 16)
        return direct(i, cf.at[chunk(p)], cf.at[chunk(p)], casend.at[i], cf_sem.at[p], (d, q))

    def start_all(make):
        lax.fori_loop(1, 16, lambda i, z: (make(i).start(), z)[1], 0)

    def drain_all(make):
        lax.fori_loop(1, 16, lambda i, z: (make(i).wait_send(), z)[1], 0)

    def wait_slots(buf, sems, me):
        def step(i, z):
            k = lax.rem(me + i, 16)
            arrived(buf.at[k], sems.at[k], None)
            return z

        lax.fori_loop(1, 16, step, 0)

    def wait_chunks(buf, sems, me):
        def step(i, z):
            k = lax.rem(me + i, 16)
            arrived(buf.at[chunk(k)], sems.at[k], None)
            return z

        lax.fori_loop(1, 16, step, 0)

    start_all(gram_copy)
    col_finish(pr, pr_sem, True)

    ph, plo = split(pr[...])
    wp4 = wp.reshape(NB, N)

    def product(j, z):
        cols = pl.ds(pl.multiple_of(j * 256, 256), 256)
        wp4[:, cols] = dot3s((ph, plo), split(s[:, cols]), PLAIN)
        return z

    lax.fori_loop(0, 4, product, 0)

    out.go(wp.at[:, 1 - c], r1, r1_sem, (row_of(zh, x, 1 - c), q))

    arrived(r1, r1_sem, None)
    t[...] = wp[:, pl.ds(c, 1)][:, 0] + r1[...]
    for phase, z in ((0, 1 - zh), (1, zh)):
        for i in (1, 3, 2):
            xx = lax.rem(x + i, 4)
            out.go(t.at[z * 4 + xx], r2.at[phase, i - 1], r2_sem.at[phase, i - 1], (row_of(zh, xx, c), q))
    wait_slots(grs, grs_sem, q)
    gf[chunk(q), :] = jnp.sum(grs[...], axis=0)
    start_all(gram_all)

    for i in (1, 3, 2):
        arrived(r2.at[0, i - 1], r2_sem.at[0, i - 1], None)
    u[...] = t[(1 - zh) * 4 + x] + (r2[0, 0] + r2[0, 1] + r2[0, 2])
    out.go(u, r3, r3_sem, (row_of(1 - zh, x, c), q))
    for i in (1, 3, 2):
        arrived(r2.at[1, i - 1], r2_sem.at[1, i - 1], None)
    part = t[zh * 4 + x] + (r2[1, 0] + r2[1, 1] + r2[1, 2])
    arrived(r3, r3_sem, None)
    mine = part + r3[...]
    wc[chunk(p), :] = mine

    for z in range(4):
        d = z * 4 + p % 4
        out.go(wc.at[chunk(p)], wr.at[chunk(p)], wr_sem.at[p], (q, d), (p != q) | (d != q))

    @pl.when(p == q)
    def _():
        wr[chunk(q), :] = mine

    row_start(wc, wc_sem, False)
    crs[pl.ds(q, 1)] = dot3(mine, pc[...], LAST)[None]
    start_all(curv_copy)
    wait_chunks(gf, gf_sem, q)
    row = lax.broadcasted_iota(jnp.int32, (NB, NB), 0)
    col = lax.broadcasted_iota(jnp.int32, (NB, NB), 1)
    aug[:, 0:NB] = gf[...]
    aug[:, NB:] = (row == col).astype(F32)
    factor_block(aug, 0)
    for i in range(4):
        k = lax.rem(zl + i, 4) * 4 + y
        arrived(wr.at[chunk(k)], wr_sem.at[k], None, (p != q) | (k != q))
        for n in (1, 3, 2):
            d = zl * 4 + lax.rem(y + n, 4)
            out.go(wr.at[chunk(k)], wr.at[chunk(k)], wr_sem.at[k], (p, d))
    row_partner(wc, wc_sem, False)
    factor_block(aug, 1)
    row_own(wc, wc_sem, False, zh)
    wait_slots(crs, crs_sem, q)
    cf[chunk(p), :] = jnp.sum(crs[...], axis=0)
    start_all(curv_all)
    factor_block(aug, 2)
    row_own(wc, wc_sem, False, 1 - zh)
    factor_block(aug, 3)
    rfac[...] = jnp.where(row <= col, aug[:, 0:NB], 0.0)
    inverse = aug[:, NB:]
    m = split(2.0 * dot6(inverse, inverse, FIRST))
    ar[...] = dot3s(m, split(pr[...]), PLAIN)
    ac[...] = dot3s(m, split(pc[...]), PLAIN)

    def put(ref, blocks, axis):
        for i, block in enumerate(blocks):
            here = slice(i * NB, (i + 1) * NB)
            if axis == 0:
                ref[here, :] = block
            else:
                ref[:, here] = block

    ah, al = split(ar[...].T)
    put(left.at[:, 0:NB], (ah,), 1)
    put(left.at[:, 2 * NB : 3 * NB], (ah,), 1)
    put(left.at[:, 4 * NB : 5 * NB], (al,), 1)
    ah, al = split(ac[...])
    put(right.at[NB : 2 * NB], (ah,), 0)
    put(right.at[3 * NB : 4 * NB], (al,), 0)
    put(right.at[5 * NB : 6 * NB], (ah,), 0)
    wait_chunks(cf, cf_sem, p)
    half = split(0.5 * cf[...])
    row_finish(wc, wc_sem, False)
    vh, vl = split(wc[...] - dot3s(half, split(ac[...]), PLAIN))
    put(right.at[0:NB], (vh,), 0)
    put(right.at[2 * NB : 3 * NB], (vl,), 0)
    put(right.at[4 * NB : 5 * NB], (vh,), 0)
    col_finish(wr, wr_sem, False)
    vh, vl = split((wr[...] - dot3s(half, split(ar[...]), PLAIN)).T)
    put(left.at[:, NB : 2 * NB], (vh,), 1)
    put(left.at[:, 3 * NB : 4 * NB], (vh,), 1)
    put(left.at[:, 5 * NB : 6 * NB], (vl,), 1)
    out.drain()
    for make in (gram_copy, gram_all, curv_copy, curv_all):
        drain_all(make)


def exchange(matrix):
    vm = pl.BlockSpec(memory_space=pltpu.VMEM)
    dma = pltpu.SemaphoreType.DMA
    big = pltpu.VMEM((NB, N), F32)
    small = pltpu.VMEM((NB, NB), F32)
    return pl.pallas_call(
        exchange_kernel,
        out_shape=(
            jax.ShapeDtypeStruct((N, 6 * NB), BF16),
            jax.ShapeDtypeStruct((6 * NB, N), BF16),
            jax.ShapeDtypeStruct((NB, NB), F32),
        ),
        in_specs=[pl.BlockSpec(memory_space=pltpu.HBM)],
        out_specs=(vm,) * 3,
        scratch_shapes=[
            big, big, big, big, small, small,
            pltpu.VMEM((N, N), F32),
            pltpu.VMEM((8, 2, CH, N), F32),
            pltpu.VMEM((8, CH, N), F32),
            pltpu.VMEM((8, CH, N), F32),
            pltpu.VMEM((2, 3, CH, N), F32),
            pltpu.VMEM((CH, N), F32),
            pltpu.VMEM((CH, N), F32),
            small,
            pltpu.VMEM((16, CH, NB), F32),
            pltpu.VMEM((16, CH, NB), F32),
            pltpu.VMEM((NB, 2 * NB), F32),
            big, big,
            dma, dma((128,)), dma((16,)), dma((16,)), dma((16,)), dma((16,)),
            dma((16,)), dma((8,)), dma((16,)), dma((16,)), dma, dma((2, 3)), dma, dma((16,)), dma((16,)), dma((16,)), dma((16,)),
        ],
        compiler_params=pltpu.CompilerParams(collective_id=0, has_side_effects=True, vmem_limit_bytes=40 << 20),
        name="exchange",
    )(matrix)


def finish_kernel(left, right, s, out):
    rows = pl.ds(pl.multiple_of(pl.program_id(0) * TILE, TILE), TILE)
    out[...] = s[...] - dot(left[rows, :], right[...], PLAIN)


TILE = 128


def finish(left, right, matrix):
    whole = lambda a: pl.BlockSpec(a.shape, lambda i: (0, 0))
    tile = pl.BlockSpec((TILE, N), lambda i: (i, 0))
    return pl.pallas_call(
        finish_kernel,
        grid=(N // TILE,),
        out_shape=jax.ShapeDtypeStruct((N, N), F32),
        in_specs=[whole(left), whole(right), tile],
        out_specs=tile,
        compiler_params=pltpu.CompilerParams(vmem_limit_bytes=32 << 20),
        name="finish",
    )(left, right, matrix)


def on_device(matrix):
    left, right, factor = exchange(matrix)
    return finish(left, right, matrix), factor


def solution(mesh):
    return jax.shard_map(
        on_device,
        mesh=mesh,
        in_specs=(P("row", "col"),),
        out_specs=(P("row", "col"), P()),
        check_vma=False,
    )
```

```python
import functools
import jax
import jax.numpy as jnp
from jax import lax
from jax.experimental import pallas as pl
from jax.experimental.pallas import tpu as pltpu
from jax.sharding import PartitionSpec as P

NB = 256
N = 1024
CH = 16
MESH = pl.DeviceIdType.MESH
F32 = jnp.float32
BF16 = jnp.bfloat16

LAST = (((1,), (1,)), ((), ()))
FIRST = (((0,), (0,)), ((), ()))
PLAIN = (((1,), (0,)), ((), ()))


def split(x):
    hi = x.astype(BF16)
    lo = (x - hi.astype(F32)).astype(BF16)
    return hi, lo


def dot(a, b, dims):
    return lax.dot_general(a, b, dims, preferred_element_type=F32)


def dot3s(a, b, dims):
    (ah, al), (bh, bl) = a, b
    return dot(ah, bh, dims) + (dot(ah, bl, dims) + dot(al, bh, dims))


def dot3(a, b, dims):
    return dot3s(split(a), split(b), dims)


def dot6(a, b, dims):
    return lax.dot_general(a, b, dims, precision=lax.Precision.HIGHEST, preferred_element_type=F32)


def chunk(k):
    return pl.ds(pl.multiple_of(k * CH, CH), CH)


class Sends:
    def __init__(self, sems):
        self.sems = sems
        self.count = 0
        self.pending = []

    def go(self, src, dst, recv, dev, cond=None):
        copy = pltpu.make_async_remote_copy(
            src_ref=src, dst_ref=dst, send_sem=self.sems.at[self.count], recv_sem=recv, device_id=dev, device_id_type=MESH
        )
        self.count += 1
        self.pending.append((copy, cond))
        when(cond, copy.start)

    def drain(self):
        for copy, cond in self.pending:
            when(cond, copy.wait_send)
        self.pending = []


def when(cond, fn):
    if cond is None:
        fn()
    else:
        pl.when(cond)(fn)


def arrived(ref, recv, cond=None):
    copy = pltpu.make_async_copy(ref, ref, recv)
    when(cond, copy.wait)


def reciprocal(x):
    y = pl.reciprocal(x, approx=True)
    return y * (2.0 - x * y)


def pivot8(step, a):
    tiles = [a[8 * t : 8 * t + 8, :] for t in range(8)]
    sub = lax.broadcasted_iota(jnp.int32, (8, 128), 0)
    full = lambda v: jnp.broadcast_to(v, (8, 128))
    cols = [[full(tile[:, i : i + 1]) for i in range(8)] for tile in tiles]
    e = [[full(cols[0][k][i : i + 1, :]) if k >= i else None for k in range(8)] for i in range(8)]
    rows = [full(tiles[0][i : i + 1, :]) for i in range(8)]
    scaled = []
    for i in range(8):
        inv = reciprocal(e[i][i])
        scaled.append(rows[i] * inv)
        for k in range(i + 1, 8):
            f = e[i][k] * inv
            rows[k] = rows[k] - f * rows[i]
            for n in range(k, 8):
                e[k][n] = e[k][n] - f * e[i][n]
            for t in range(1, 8):
                cols[t][k] = cols[t][k] - cols[t][i] * f
    top = rows[0]
    for i in range(1, 8):
        top = jnp.where(sub == i, rows[i], top)
    new = []
    for t in range(1, 8):
        term = cols[t][0] * scaled[0]
        for i in range(1, 8):
            term = term + cols[t][i] * scaled[i]
        new.append(tiles[t] - term * jnp.where(step + t < 8, 1.0, 0.0).astype(F32))
    return pltpu.roll(jnp.concatenate(new + [top], axis=0), 120, axis=1)


def factor_block(aug, k):
    b = 64
    row = lax.broadcasted_iota(jnp.int32, (b, 2 * b), 0)
    col = lax.broadcasted_iota(jnp.int32, (b, 2 * b), 1)
    here = slice(k * b, (k + 1) * b)
    eye = (row + b == col).astype(F32)
    a = jnp.concatenate([aug[here, here], eye[:, b:]], axis=1)
    a = lax.fori_loop(0, 8, pivot8, a)
    diag = jnp.sum(jnp.where(row + b == col, a, 0.0), axis=1, keepdims=True)
    inverse = (a * lax.rsqrt(diag))[:, :b]
    done = dot6(inverse, aug[here, :], PLAIN)
    aug[here, :] = done
    if k < 3:
        below = slice((k + 1) * b, NB)
        aug[below, :] = aug[below, :] - dot6(done[:, (k + 1) * b : NB], done, FIRST)


def exchange_kernel(
    s_hbm, left, right, rfac,
    pr, pc, wr, wc, gf, cf, s, wp, r1, t, r2, u, r3, gp, grs, crs, aug, ac,
    load_sem, send_sem, gsend, gasend, csend, casend,
    pr_sem, pc_sem, wr_sem, wc_sem, r1_sem, r2_sem, r3_sem, grs_sem, gf_sem, crs_sem, cf_sem,
):
    p = lax.axis_index("row")
    q = lax.axis_index("col")
    zh, x, c = p // 8, (p // 2) % 4, p % 2
    zl, y = q // 4, q % 4
    same = p == q
    j = x * 2 + c

    load = pltpu.make_async_copy(s_hbm, s, load_sem)
    load.start()

    barrier = pltpu.get_barrier_semaphore()

    def hello(dev):
        pl.semaphore_signal(barrier, inc=1, device_id=dev, device_id_type=MESH)

    def greet(i, carry):
        hello((lax.rem(p + i, 16), q))
        hello((p, lax.rem(q + i, 16)))
        return carry

    lax.fori_loop(1, 16, greet, 0)
    pl.semaphore_wait(barrier, 30)
    load.wait()
    out = Sends(send_sem)

    def send_chunk(buf, sems, k, dev, cond=None):
        out.go(buf.at[chunk(k)], buf.at[chunk(k)], sems.at[k], dev, cond)

    def wait_chunk(buf, sems, k, cond=None):
        arrived(buf.at[chunk(k)], sems.at[k], cond)


    def col_of(i, n):
        return lax.rem(zl + i, 4) * 4 + lax.rem(y + n, 4)

    def col_z(buf, sems, root):
        for i in (1, 3, 2):
            d = col_of(i, 0)
            send_chunk(buf, sems, q, (p, d), (d != 0) if root else None)

    def col_y(buf, sems, root, i):
        k = col_of(i, 0)
        if i:
            wait_chunk(buf, sems, k, (q != 0) if root else None)
        for n in (1, 3, 2):
            d = col_of(0, n)
            send_chunk(buf, sems, k, (p, d), (d != 0) if root else None)

    def col_finish(buf, sems, root):
        for i in (0, 1, 3, 2):
            for n in (1, 3, 2):
                wait_chunk(buf, sems, col_of(i, n), (q != 0) if root else None)


    def pair_send(buf, sems, k, d, cond):
        view = buf.reshape(2, 8, CH, N)
        out.go(view.at[:, k], view.at[:, k], sems.at[k], (d, q), cond)

    def pair_wait(buf, sems, k, cond):
        arrived(buf.reshape(2, 8, CH, N).at[:, k], sems.at[k], cond)

    def pair_spread(buf, sems, here):
        for i in (1, 3, 2):
            d = zh * 8 + lax.rem(x + i, 4) * 2 + c
            pair_send(buf, sems, j, d, here & (d != 0))
        d = zh * 8 + x * 2 + 1 - c
        pair_send(buf, sems, j, d, here & (d != 0))

    def pair_forward(buf, sems, root):
        d = zh * 8 + x * 2 + 1 - c
        for i in (1, 3, 2):
            k = lax.rem(x + i, 4) * 2 + c
            pair_wait(buf, sems, k, (p != 0) if root else None)
            pair_send(buf, sems, k, d, (d != 0) if root else None)

    def pair_finish(buf, sems, root):
        for i in (0, 1, 3, 2):
            pair_wait(buf, sems, lax.rem(x + i, 4) * 2 + 1 - c, (p != 0) if root else None)


    def row_of(z, i, core):
        return z * 8 + lax.rem(x + i, 4) * 2 + core

    def row_spread(buf, sems, k):
        for i in (1, 3, 2):
            send_chunk(buf, sems, k, (row_of(zh, i, c), q))
        send_chunk(buf, sems, k, (row_of(zh, 0, 1 - c), q))

    def row_start(buf, sems):
        send_chunk(buf, sems, p, (row_of(1 - zh, 0, c), q))
        row_spread(buf, sems, p)

    def row_partner(buf, sems):
        k = row_of(1 - zh, 0, c)
        wait_chunk(buf, sems, k)
        row_spread(buf, sems, k)

    def row_own(buf, sems, z):
        for i in (1, 3, 2):
            k = row_of(z, i, c)
            wait_chunk(buf, sems, k)
            send_chunk(buf, sems, k, (row_of(zh, 0, 1 - c), q))

    def row_finish(buf, sems):
        for z in (zh, 1 - zh):
            for i in (0, 1, 3, 2):
                wait_chunk(buf, sems, row_of(z, i, 1 - c))


    def direct(src, dst, ssem, rsem, dev):
        return pltpu.make_async_remote_copy(
            src_ref=src, dst_ref=dst, send_sem=ssem, recv_sem=rsem, device_id=dev, device_id_type=MESH
        )

    def gram_copy(i):
        d = lax.rem(q + i, 16)
        return direct(gp.at[chunk(d)], grs.at[q], gsend.at[i], grs_sem.at[q], (p, d))

    def gram_all(i):
        d = lax.rem(q + i, 16)
        return direct(gf.at[chunk(q)], gf.at[chunk(q)], gasend.at[i], gf_sem.at[q], (p, d))

    def curv_copy(i):
        d = lax.rem(q + i, 16)
        return direct(crs.at[q], crs.at[q], csend.at[i], crs_sem.at[q], (p, d))

    def curv_all(i):
        d = lax.rem(p + i, 16)
        return direct(cf.at[chunk(p)], cf.at[chunk(p)], casend.at[i], cf_sem.at[p], (d, q))

    def start_all(make):
        lax.fori_loop(1, 16, lambda i, z: (make(i).start(), z)[1], 0)

    def drain_all(make):
        lax.fori_loop(1, 16, lambda i, z: (make(i).wait_send(), z)[1], 0)

    def wait_slots(buf, sems, me):
        def step(i, z):
            k = lax.rem(me + i, 16)
            arrived(buf.at[k], sems.at[k])
            return z

        lax.fori_loop(1, 16, step, 0)

    def wait_chunks(buf, sems, me):
        def step(i, z):
            wait_chunk(buf, sems, lax.rem(me + i, 16))
            return z

        lax.fori_loop(1, 16, step, 0)

    lane = lax.broadcasted_iota(jnp.int32, (NB, N), 1)

    @pl.when(p == 0)
    def _():
        pc[...] = jnp.where((q == 0) & (lane < NB), 0.0, s[0:NB, :])

    for k in (4, 5, 2, 3, 6, 7, 1):
        pair_send(pc, pc_sem, k, k, p == 0)

    @pl.when(q == 0)
    def _():
        pr[...] = jnp.where((p == 0) & (lane < NB), 0.0, s[:, 0:NB].T)

    for i in range(4):
        for n in (1, 3, 2):
            send_chunk(pr, pr_sem, i * 4 + n, (p, n), q == 0)

    def line(i, here):
        k = i * 4 + y
        wait_chunk(pr, pr_sem, k, here & (q != 0))
        send_chunk(pr, pr_sem, k, (p, lax.rem(q + 4, 16)), here & (zl < 3))
        for n in (1, 3, 2):
            d = col_of(0, n)
            send_chunk(pr, pr_sem, k, (p, d), here & (d != 0))

    near, far, first = zh == 0, zh == 1, zl == 0
    line(0, first)
    pair_wait(pc, pc_sem, j, near & (p != 0))
    pair_send(pc, pc_sem, j, 8 + j, near)
    pair_spread(pc, pc_sem, near)
    line(0, zl > 0)
    line(1, zl >= 0)
    pair_wait(pc, pc_sem, j, far)
    pair_spread(pc, pc_sem, far)
    line(2, zl >= 0)
    line(3, zl >= 0)
    pair_forward(pc, pc_sem, True)
    pair_finish(pc, pc_sem, True)

    pch, pcl = split(pc[...])
    gp[...] = dot3s((pch, pcl), (pch, pcl), LAST)
    grs[pl.ds(q, 1)] = gp[chunk(q), :][None]
    start_all(gram_copy)

    col_finish(pr, pr_sem, True)
    prh, prl = split(pr[...])

    def product(i, z):
        cols = pl.ds(pl.multiple_of(i * 256, 256), 256)
        wp.reshape(NB, N)[:, cols] = dot3s((prh, prl), split(s[:, cols]), PLAIN)
        return z

    lax.fori_loop(0, 4, product, 0)

    out.go(wp.at[:, 1 - c], r1, r1_sem, (zh * 8 + x * 2 + 1 - c, q))
    wait_slots(grs, grs_sem, q)
    gf[chunk(q), :] = jnp.sum(grs[...], axis=0)
    start_all(gram_all)
    arrived(r1, r1_sem)
    t[...] = wp[:, pl.ds(c, 1)][:, 0] + r1[...]
    for phase, z in ((0, 1 - zh), (1, zh)):
        for i in (1, 3, 2):
            xx = lax.rem(x + i, 4)
            out.go(t.at[z * 4 + xx], r2.at[phase, i - 1], r2_sem.at[phase, i - 1], (zh * 8 + xx * 2 + c, q))
    for i in (1, 3, 2):
        arrived(r2.at[0, i - 1], r2_sem.at[0, i - 1])
    u[...] = t[(1 - zh) * 4 + x] + (r2[0, 0] + r2[0, 1] + r2[0, 2])
    out.go(u, r3, r3_sem, ((1 - zh) * 8 + j, q))
    wait_chunks(gf, gf_sem, q)
    row = lax.broadcasted_iota(jnp.int32, (NB, NB), 0)
    col = lax.broadcasted_iota(jnp.int32, (NB, NB), 1)
    aug[:, 0:NB] = gf[...]
    aug[:, NB:] = (row == col).astype(F32)
    factor_block(aug, 0)
    for i in (1, 3, 2):
        arrived(r2.at[1, i - 1], r2_sem.at[1, i - 1])
    part = t[zh * 4 + x] + (r2[1, 0] + r2[1, 1] + r2[1, 2])
    arrived(r3, r3_sem)
    mine = part + r3[...]
    wc[chunk(p), :] = mine

    out.go(wc.at[chunk(p)], wr.at[chunk(p)], wr_sem.at[p], (q, p), p != q)
    row_start(wc, wc_sem)

    @pl.when(same)
    def _():
        wr[chunk(q), :] = mine

    crs[pl.ds(q, 1)] = dot3s(split(mine), (pch, pcl), LAST)[None]
    start_all(curv_copy)
    factor_block(aug, 1)
    wait_chunk(wr, wr_sem, q, p != q)
    col_z(wr, wr_sem, False)
    col_y(wr, wr_sem, False, 0)
    row_partner(wc, wc_sem)
    factor_block(aug, 2)
    for i in (1, 3, 2):
        col_y(wr, wr_sem, False, i)
    row_own(wc, wc_sem, zh)
    wait_slots(crs, crs_sem, q)
    cf[chunk(p), :] = jnp.sum(crs[...], axis=0)
    start_all(curv_all)
    factor_block(aug, 3)
    row_own(wc, wc_sem, 1 - zh)
    rfac[...] = jnp.where(row <= col, aug[:, 0:NB], 0.0)
    inverse = aug[:, NB:]
    m = split(2.0 * dot6(inverse, inverse, FIRST))
    ac[...] = dot3s(m, split(pc[...]), PLAIN)
    ah, al = split(ac[...])
    right[NB : 2 * NB, :] = ah
    right[3 * NB : 4 * NB, :] = al
    rh, rl = split(dot3s(m, split(pr[...]), PLAIN).T)
    left[:, 0:NB] = rh
    left[:, 2 * NB : 3 * NB] = rl

    wait_chunks(cf, cf_sem, p)
    turned = dot3s(split(cf[...]), (ah, al), PLAIN)
    row_finish(wc, wc_sem)
    vh, vl = split(wc[...] - turned)
    right[0:NB, :] = vh
    right[2 * NB : 3 * NB, :] = vl
    col_finish(wr, wr_sem, False)
    vh, vl = split(wr[...].T)
    left[:, NB : 2 * NB] = vh
    left[:, 3 * NB : 4 * NB] = vl
    out.drain()
    for make in (gram_copy, gram_all, curv_copy, curv_all):
        drain_all(make)


def exchange(matrix):
    vm = pl.BlockSpec(memory_space=pltpu.VMEM)
    dma = pltpu.SemaphoreType.DMA
    big = pltpu.VMEM((NB, N), F32)
    small = pltpu.VMEM((NB, NB), F32)
    return pl.pallas_call(
        exchange_kernel,
        out_shape=(
            jax.ShapeDtypeStruct((N, 4 * NB), BF16),
            jax.ShapeDtypeStruct((4 * NB, N), BF16),
            jax.ShapeDtypeStruct((NB, NB), F32),
        ),
        in_specs=[pl.BlockSpec(memory_space=pltpu.HBM)],
        out_specs=(vm,) * 3,
        scratch_shapes=[
            big, big, big, big, small, small,
            pltpu.VMEM((N, N), F32),
            pltpu.VMEM((8, 2, CH, N), F32),
            pltpu.VMEM((8, CH, N), F32),
            pltpu.VMEM((8, CH, N), F32),
            pltpu.VMEM((2, 3, CH, N), F32),
            pltpu.VMEM((CH, N), F32),
            pltpu.VMEM((CH, N), F32),
            small,
            pltpu.VMEM((16, CH, NB), F32),
            pltpu.VMEM((16, CH, NB), F32),
            pltpu.VMEM((NB, 2 * NB), F32),
            big,
            dma, dma((96,)), dma((16,)), dma((16,)), dma((16,)), dma((16,)),
            dma((16,)), dma((8,)), dma((16,)), dma((16,)), dma, dma((2, 3)), dma,
            dma((16,)), dma((16,)), dma((16,)), dma((16,)),
        ],
        compiler_params=pltpu.CompilerParams(collective_id=0, has_side_effects=True, vmem_limit_bytes=48 << 20),
        name="exchange",
    )(matrix)


def finish_kernel(left, right, factor, s, out, r):
    rows = pl.ds(pl.multiple_of(pl.program_id(0) * TILE, TILE), TILE)
    half = 2 * NB
    lh, ll = left[rows, 0:half], left[rows, half:]
    rh, rl = right[0:half, :], right[half:, :]
    out[...] = s[...] - (dot(lh, rh, PLAIN) + (dot(lh, rl, PLAIN) + dot(ll, rh, PLAIN)))
    r[...] = factor[...]


TILE = 128


def finish(left, right, factor, matrix):
    whole = lambda a: pl.BlockSpec(a.shape, lambda i: (0, 0))
    tile = pl.BlockSpec((TILE, N), lambda i: (i, 0))
    return pl.pallas_call(
        finish_kernel,
        grid=(N // TILE,),
        out_shape=(jax.ShapeDtypeStruct((N, N), F32), jax.ShapeDtypeStruct((NB, NB), F32)),
        in_specs=[whole(left), whole(right), whole(factor), tile],
        out_specs=(tile, whole(factor)),
        compiler_params=pltpu.CompilerParams(vmem_limit_bytes=32 << 20),
        name="finish",
    )(left, right, factor, matrix)


def on_device(matrix):
    return finish(*exchange(matrix), matrix)


def solution(mesh):
    return jax.shard_map(
        on_device,
        mesh=mesh,
        in_specs=(P("row", "col"),),
        out_specs=(P("row", "col"), P()),
        check_vma=False,
    )
```

```python
import functools
import jax
import jax.numpy as jnp
from jax import lax
from jax.experimental import pallas as pl
from jax.experimental.pallas import tpu as pltpu
from jax.sharding import PartitionSpec as P

NB = 256
N = 1024
CH = 16
MESH = pl.DeviceIdType.MESH
F32 = jnp.float32
BF16 = jnp.bfloat16

LAST = (((1,), (1,)), ((), ()))
FIRST = (((0,), (0,)), ((), ()))
PLAIN = (((1,), (0,)), ((), ()))


def split(x):
    hi = x.astype(BF16)
    lo = (x - hi.astype(F32)).astype(BF16)
    return hi, lo


def dot(a, b, dims):
    return lax.dot_general(a, b, dims, preferred_element_type=F32)


def dot3s(a, b, dims):
    (ah, al), (bh, bl) = a, b
    return dot(ah, bh, dims) + (dot(ah, bl, dims) + dot(al, bh, dims))


def dot3(a, b, dims):
    return dot3s(split(a), split(b), dims)


def dot6(a, b, dims):
    return lax.dot_general(a, b, dims, precision=lax.Precision.HIGHEST, preferred_element_type=F32)


def chunk(k):
    return pl.ds(pl.multiple_of(k * CH, CH), CH)


class Sends:
    def __init__(self, sems):
        self.sems = sems
        self.count = 0
        self.pending = []

    def go(self, src, dst, recv, dev, cond=None):
        copy = pltpu.make_async_remote_copy(
            src_ref=src, dst_ref=dst, send_sem=self.sems.at[self.count], recv_sem=recv, device_id=dev, device_id_type=MESH
        )
        self.count += 1
        self.pending.append((copy, cond))
        when(cond, copy.start)

    def drain(self):
        for copy, cond in self.pending:
            when(cond, copy.wait_send)
        self.pending = []


def when(cond, fn):
    if cond is None:
        fn()
    else:
        pl.when(cond)(fn)


def arrived(ref, recv, cond=None):
    copy = pltpu.make_async_copy(ref, ref, recv)
    when(cond, copy.wait)


def reciprocal(x):
    y = pl.reciprocal(x, approx=True)
    return y * (2.0 - x * y)


def pivot8(step, a):
    tiles = [a[8 * t : 8 * t + 8, :] for t in range(8)]
    sub = lax.broadcasted_iota(jnp.int32, (8, 128), 0)
    full = lambda v: jnp.broadcast_to(v, (8, 128))
    cols = [[full(tile[:, i : i + 1]) for i in range(8)] for tile in tiles]
    e = [[full(cols[0][k][i : i + 1, :]) if k >= i else None for k in range(8)] for i in range(8)]
    rows = [full(tiles[0][i : i + 1, :]) for i in range(8)]
    scaled = []
    for i in range(8):
        inv = reciprocal(e[i][i])
        scaled.append(rows[i] * inv)
        for k in range(i + 1, 8):
            f = e[i][k] * inv
            rows[k] = rows[k] - f * rows[i]
            for n in range(k, 8):
                e[k][n] = e[k][n] - f * e[i][n]
            for t in range(1, 8):
                cols[t][k] = cols[t][k] - cols[t][i] * f
    top = rows[0]
    for i in range(1, 8):
        top = jnp.where(sub == i, rows[i], top)
    new = []
    for t in range(1, 8):
        term = cols[t][0] * scaled[0]
        for i in range(1, 8):
            term = term + cols[t][i] * scaled[i]
        new.append(tiles[t] - term * jnp.where(step + t < 8, 1.0, 0.0).astype(F32))
    return pltpu.roll(jnp.concatenate(new + [top], axis=0), 120, axis=1)


def factor_block(aug, k):
    b = 64
    row = lax.broadcasted_iota(jnp.int32, (b, 2 * b), 0)
    col = lax.broadcasted_iota(jnp.int32, (b, 2 * b), 1)
    here = slice(k * b, (k + 1) * b)
    eye = (row + b == col).astype(F32)
    a = jnp.concatenate([aug[here, here], eye[:, b:]], axis=1)
    a = lax.fori_loop(0, 8, pivot8, a)
    diag = jnp.sum(jnp.where(row + b == col, a, 0.0), axis=1, keepdims=True)
    inverse = (a * lax.rsqrt(diag))[:, :b]
    done = dot6(inverse, aug[here, :], PLAIN)
    aug[here, :] = done
    if k < 3:
        below = slice((k + 1) * b, NB)
        aug[below, :] = aug[below, :] - dot6(done[:, (k + 1) * b : NB], done, FIRST)


def exchange_kernel(
    s_hbm, left, right, rfac,
    pr, pc, wr, wc, gf, cf, s, wp, r1, t, r2, u, r3, gp, grs, c0, c1, cy, cz, aug, ac,
    load_sem, send_sem, gsend, gdsend, gasend,
    pr_sem, pc_sem, wr_sem, wc_sem, r1_sem, r2_sem, r3_sem, grs_sem, gf_sem, cy_sem, cz_sem, cf_sem,
):
    p = lax.axis_index("row")
    q = lax.axis_index("col")
    zh, x, c = p // 8, (p // 2) % 4, p % 2
    zl, y = q // 4, q % 4
    same = p == q
    j = x * 2 + c

    load = pltpu.make_async_copy(s_hbm, s, load_sem)
    load.start()

    barrier = pltpu.get_barrier_semaphore()

    def hello(dev):
        pl.semaphore_signal(barrier, inc=1, device_id=dev, device_id_type=MESH)

    def greet(i, carry):
        hello((lax.rem(p + i, 16), q))
        hello((p, lax.rem(q + i, 16)))
        return carry

    lax.fori_loop(1, 16, greet, 0)
    pl.semaphore_wait(barrier, 30)
    load.wait()
    out = Sends(send_sem)

    def send_chunk(buf, sems, k, dev, cond=None):
        out.go(buf.at[chunk(k)], buf.at[chunk(k)], sems.at[k], dev, cond)

    def wait_chunk(buf, sems, k, cond=None):
        arrived(buf.at[chunk(k)], sems.at[k], cond)


    def col_of(i, n):
        return lax.rem(zl + i, 4) * 4 + lax.rem(y + n, 4)

    def col_z(buf, sems, root):
        for i in (1, 3, 2):
            d = col_of(i, 0)
            send_chunk(buf, sems, q, (p, d), (d != 0) if root else None)

    def col_y(buf, sems, root, i):
        k = col_of(i, 0)
        if i:
            wait_chunk(buf, sems, k, (q != 0) if root else None)
        for n in (1, 3, 2):
            d = col_of(0, n)
            send_chunk(buf, sems, k, (p, d), (d != 0) if root else None)

    def col_finish(buf, sems, root):
        for i in (0, 1, 3, 2):
            for n in (1, 3, 2):
                wait_chunk(buf, sems, col_of(i, n), (q != 0) if root else None)


    def pair_send(buf, sems, k, d, cond):
        view = buf.reshape(2, 8, CH, N)
        out.go(view.at[:, k], view.at[:, k], sems.at[k], (d, q), cond)

    def pair_wait(buf, sems, k, cond):
        arrived(buf.reshape(2, 8, CH, N).at[:, k], sems.at[k], cond)

    def pair_spread(buf, sems, here):
        for i in (1, 3, 2):
            d = zh * 8 + lax.rem(x + i, 4) * 2 + c
            pair_send(buf, sems, j, d, here & (d != 0))
        d = zh * 8 + x * 2 + 1 - c
        pair_send(buf, sems, j, d, here & (d != 0))

    def pair_forward(buf, sems, root):
        d = zh * 8 + x * 2 + 1 - c
        for i in (1, 3, 2):
            k = lax.rem(x + i, 4) * 2 + c
            pair_wait(buf, sems, k, (p != 0) if root else None)
            pair_send(buf, sems, k, d, (d != 0) if root else None)

    def pair_finish(buf, sems, root):
        for i in (0, 1, 3, 2):
            pair_wait(buf, sems, lax.rem(x + i, 4) * 2 + 1 - c, (p != 0) if root else None)


    def row_of(z, i, core):
        return z * 8 + lax.rem(x + i, 4) * 2 + core

    def row_spread(buf, sems, k):
        for i in (1, 3, 2):
            send_chunk(buf, sems, k, (row_of(zh, i, c), q))
        send_chunk(buf, sems, k, (row_of(zh, 0, 1 - c), q))

    def row_start(buf, sems):
        send_chunk(buf, sems, p, (row_of(1 - zh, 0, c), q))
        row_spread(buf, sems, p)

    def row_partner(buf, sems):
        k = row_of(1 - zh, 0, c)
        wait_chunk(buf, sems, k)
        row_spread(buf, sems, k)

    def row_own(buf, sems, z):
        for i in (1, 3, 2):
            k = row_of(z, i, c)
            wait_chunk(buf, sems, k)
            send_chunk(buf, sems, k, (row_of(zh, 0, 1 - c), q))

    def row_finish(buf, sems):
        for z in (zh, 1 - zh):
            for i in (0, 1, 3, 2):
                wait_chunk(buf, sems, row_of(z, i, 1 - c))


    def direct(src, dst, ssem, rsem, dev):
        return pltpu.make_async_remote_copy(
            src_ref=src, dst_ref=dst, send_sem=ssem, recv_sem=rsem, device_id=dev, device_id_type=MESH
        )

    def gram_copy(i):
        d = lax.rem(q + i, 16)
        return direct(gp.at[chunk(d)], grs.at[q], gsend.at[i], grs_sem.at[q], (p, d))

    def gram_all(i):
        d = lax.rem(q + i, 16)
        return direct(gf.at[chunk(q)], gf.at[chunk(q)], gasend.at[i], gf_sem.at[q], (p, d))

    def gram_down(i):
        return direct(gf.at[chunk(q)], gf.at[chunk(q)], gdsend.at[i], gf_sem.at[q], (i, q))

    def start_all(make):
        lax.fori_loop(1, 16, lambda i, z: (make(i).start(), z)[1], 0)

    def drain_all(make):
        lax.fori_loop(1, 16, lambda i, z: (make(i).wait_send(), z)[1], 0)

    def wait_slots(buf, sems, me):
        def step(i, z):
            k = lax.rem(me + i, 16)
            arrived(buf.at[k], sems.at[k])
            return z

        lax.fori_loop(1, 16, step, 0)

    def wait_chunks(buf, sems, me):
        def step(i, z):
            wait_chunk(buf, sems, lax.rem(me + i, 16))
            return z

        lax.fori_loop(1, 16, step, 0)

    lane = lax.broadcasted_iota(jnp.int32, (NB, N), 1)

    @pl.when(p == 0)
    def _():
        pc[...] = jnp.where((q == 0) & (lane < NB), 0.0, s[0:NB, :])

    for k in (4, 5, 2, 3, 6, 7, 1):
        pair_send(pc, pc_sem, k, k, p == 0)

    @pl.when(p == 0)
    def _():
        both = split(pc[...])
        gp[...] = dot3s(both, both, LAST)
        grs[pl.ds(q, 1)] = gp[chunk(q), :][None]
        start_all(gram_copy)

    @pl.when(q == 0)
    def _():
        pr[...] = jnp.where((p == 0) & (lane < NB), 0.0, s[:, 0:NB].T)

    for i in range(4):
        for n in (1, 3, 2):
            send_chunk(pr, pr_sem, i * 4 + n, (p, n), q == 0)

    def line(i, here):
        k = i * 4 + y
        wait_chunk(pr, pr_sem, k, here & (q != 0))
        send_chunk(pr, pr_sem, k, (p, lax.rem(q + 4, 16)), here & (zl < 3))
        for n in (1, 3, 2):
            d = col_of(0, n)
            send_chunk(pr, pr_sem, k, (p, d), here & (d != 0))

    near, far, first = zh == 0, zh == 1, zl == 0
    line(0, first)
    pair_wait(pc, pc_sem, j, near & (p != 0))
    pair_send(pc, pc_sem, j, 8 + j, near)
    pair_spread(pc, pc_sem, near)
    line(0, zl > 0)
    line(1, zl >= 0)

    @pl.when(p == 0)
    def _():
        wait_slots(grs, grs_sem, q)
        gf[chunk(q), :] = jnp.sum(grs[...], axis=0)
        start_all(gram_down)

    pair_wait(pc, pc_sem, j, far)
    pair_spread(pc, pc_sem, far)
    line(2, zl >= 0)
    line(3, zl >= 0)
    pair_forward(pc, pc_sem, True)
    pair_finish(pc, pc_sem, True)
    wait_chunk(gf, gf_sem, q, p != 0)
    start_all(gram_all)

    col_finish(pr, pr_sem, True)
    prh, prl = split(pr[...])

    def product(i, z):
        cols = pl.ds(pl.multiple_of(i * 256, 256), 256)
        wp.reshape(NB, N)[:, cols] = dot3s((prh, prl), split(s[:, cols]), PLAIN)
        return z

    lax.fori_loop(0, 4, product, 0)

    out.go(wp.at[:, 1 - c], r1, r1_sem, (zh * 8 + x * 2 + 1 - c, q))
    arrived(r1, r1_sem)
    t[...] = wp[:, pl.ds(c, 1)][:, 0] + r1[...]
    for phase, z in ((0, 1 - zh), (1, zh)):
        for i in (1, 3, 2):
            xx = lax.rem(x + i, 4)
            out.go(t.at[z * 4 + xx], r2.at[phase, i - 1], r2_sem.at[phase, i - 1], (zh * 8 + xx * 2 + c, q))
    wait_chunks(gf, gf_sem, q)
    row = lax.broadcasted_iota(jnp.int32, (NB, NB), 0)
    col = lax.broadcasted_iota(jnp.int32, (NB, NB), 1)
    aug[:, 0:NB] = gf[...]
    aug[:, NB:] = (row == col).astype(F32)
    factor_block(aug, 0)
    factor_block(aug, 1)
    for i in (1, 3, 2):
        arrived(r2.at[0, i - 1], r2_sem.at[0, i - 1])
    u[...] = t[(1 - zh) * 4 + x] + (r2[0, 0] + r2[0, 1] + r2[0, 2])
    out.go(u, r3, r3_sem, ((1 - zh) * 8 + j, q))
    factor_block(aug, 2)
    for i in (1, 3, 2):
        arrived(r2.at[1, i - 1], r2_sem.at[1, i - 1])
    part = t[zh * 4 + x] + (r2[1, 0] + r2[1, 1] + r2[1, 2])
    arrived(r3, r3_sem)
    mine = part + r3[...]
    wc[chunk(p), :] = mine

    curv = cf.reshape(2, 4, 2, CH, NB)
    c0[...] = dot3(mine, pc[...], LAST)
    for i in (1, 3, 2):
        out.go(c0, cy.at[i - 1], cy_sem.at[i - 1], (p, col_of(0, i)))
    out.go(wc.at[chunk(p)], wr.at[chunk(p)], wr_sem.at[p], (q, p), p != q)
    row_start(wc, wc_sem)

    @pl.when(same)
    def _():
        wr[chunk(q), :] = mine

    for i in (1, 3, 2):
        arrived(cy.at[i - 1], cy_sem.at[i - 1])
    c1[...] = c0[...] + (cy[0] + cy[1] + cy[2])
    for i in (1, 3, 2):
        out.go(c1, cz.at[i - 1], cz_sem.at[i - 1], (p, col_of(i, 0)))
    factor_block(aug, 3)
    wait_chunk(wr, wr_sem, q, p != q)
    col_z(wr, wr_sem, False)
    col_y(wr, wr_sem, False, 0)
    for i in (1, 3, 2):
        arrived(cz.at[i - 1], cz_sem.at[i - 1])
    cf[chunk(p), :] = c1[...] + (cz[0] + cz[1] + cz[2])
    out.go(cf.at[chunk(p)], cf.at[chunk(p)], cf_sem.at[0], (row_of(1 - zh, 0, c), q))
    row_partner(wc, wc_sem)
    rfac[...] = jnp.where(row <= col, aug[:, 0:NB], 0.0)
    inverse = aug[:, NB:]
    m = split(2.0 * dot6(inverse, inverse, FIRST))
    ac[...] = dot3s(m, split(pc[...]), PLAIN)
    ah, al = split(ac[...])
    right[NB : 2 * NB, :] = ah
    right[3 * NB : 4 * NB, :] = al
    for i in (1, 3, 2):
        col_y(wr, wr_sem, False, i)
    arrived(cf.at[chunk(row_of(1 - zh, 0, c))], cf_sem.at[0])
    for i in (1, 3, 2):
        out.go(curv.at[:, x, c], curv.at[:, x, c], cf_sem.at[i], (row_of(zh, i, c), q))
    row_own(wc, wc_sem, zh)
    rh, rl = split(dot3s(m, split(pr[...]), PLAIN).T)
    left[:, 0:NB] = rh
    left[:, 2 * NB : 3 * NB] = rl
    for i in (1, 3, 2):
        arrived(curv.at[:, lax.rem(x + 4 - i, 4), c], cf_sem.at[i])
    out.go(curv.at[:, :, c], curv.at[:, :, c], cf_sem.at[4], (row_of(zh, 0, 1 - c), q))
    row_own(wc, wc_sem, 1 - zh)
    arrived(curv.at[:, :, 1 - c], cf_sem.at[4])

    turned = dot3s(split(cf[...]), (ah, al), PLAIN)
    row_finish(wc, wc_sem)
    vh, vl = split(wc[...] - turned)
    right[0:NB, :] = vh
    right[2 * NB : 3 * NB, :] = vl
    col_finish(wr, wr_sem, False)
    vh, vl = split(wr[...].T)
    left[:, NB : 2 * NB] = vh
    left[:, 3 * NB : 4 * NB] = vl
    out.drain()

    @pl.when(p == 0)
    def _():
        drain_all(gram_copy)
        drain_all(gram_down)

    drain_all(gram_all)


def exchange(matrix):
    vm = pl.BlockSpec(memory_space=pltpu.VMEM)
    dma = pltpu.SemaphoreType.DMA
    big = pltpu.VMEM((NB, N), F32)
    small = pltpu.VMEM((NB, NB), F32)
    return pl.pallas_call(
        exchange_kernel,
        out_shape=(
            jax.ShapeDtypeStruct((N, 4 * NB), BF16),
            jax.ShapeDtypeStruct((4 * NB, N), BF16),
            jax.ShapeDtypeStruct((NB, NB), F32),
        ),
        in_specs=[pl.BlockSpec(memory_space=pltpu.HBM)],
        out_specs=(vm,) * 3,
        scratch_shapes=[
            big, big, big, big, small, small,
            pltpu.VMEM((N, N), F32),
            pltpu.VMEM((8, 2, CH, N), F32),
            pltpu.VMEM((8, CH, N), F32),
            pltpu.VMEM((8, CH, N), F32),
            pltpu.VMEM((2, 3, CH, N), F32),
            pltpu.VMEM((CH, N), F32),
            pltpu.VMEM((CH, N), F32),
            small,
            pltpu.VMEM((16, CH, NB), F32),
            pltpu.VMEM((CH, NB), F32),
            pltpu.VMEM((CH, NB), F32),
            pltpu.VMEM((3, CH, NB), F32),
            pltpu.VMEM((3, CH, NB), F32),
            pltpu.VMEM((NB, 2 * NB), F32),
            big,
            dma, dma((112,)), dma((16,)), dma((16,)), dma((16,)),
            dma((16,)), dma((8,)), dma((16,)), dma((16,)), dma, dma((2, 3)), dma,
            dma((16,)), dma((16,)), dma((3,)), dma((3,)), dma((5,)),
        ],
        compiler_params=pltpu.CompilerParams(collective_id=0, has_side_effects=True, vmem_limit_bytes=48 << 20),
        name="exchange",
    )(matrix)


def finish_kernel(left, right, factor, s, out, r):
    rows = pl.ds(pl.multiple_of(pl.program_id(0) * TILE, TILE), TILE)
    half = 2 * NB
    lh, ll = left[rows, 0:half], left[rows, half:]
    rh, rl = right[0:half, :], right[half:, :]
    out[...] = s[...] - (dot(lh, rh, PLAIN) + (dot(lh, rl, PLAIN) + dot(ll, rh, PLAIN)))
    r[...] = factor[...]


TILE = 128


def finish(left, right, factor, matrix):
    whole = lambda a: pl.BlockSpec(a.shape, lambda i: (0, 0))
    tile = pl.BlockSpec((TILE, N), lambda i: (i, 0))
    return pl.pallas_call(
        finish_kernel,
        grid=(N // TILE,),
        out_shape=(jax.ShapeDtypeStruct((N, N), F32), jax.ShapeDtypeStruct((NB, NB), F32)),
        in_specs=[whole(left), whole(right), whole(factor), tile],
        out_specs=(tile, whole(factor)),
        compiler_params=pltpu.CompilerParams(vmem_limit_bytes=32 << 20),
        name="finish",
    )(left, right, factor, matrix)


def on_device(matrix):
    return finish(*exchange(matrix), matrix)


def solution(mesh):
    return jax.shard_map(
        on_device,
        mesh=mesh,
        in_specs=(P("row", "col"),),
        out_specs=(P("row", "col"), P()),
        check_vma=False,
    )
```

```python
import functools
import jax
import jax.numpy as jnp
from jax import lax
from jax.experimental import pallas as pl
from jax.experimental.pallas import tpu as pltpu
from jax.sharding import PartitionSpec as P

NB = 256
N = 1024
CH = 16
MESH = pl.DeviceIdType.MESH
F32 = jnp.float32
BF16 = jnp.bfloat16

LAST = (((1,), (1,)), ((), ()))
FIRST = (((0,), (0,)), ((), ()))
PLAIN = (((1,), (0,)), ((), ()))


def split(x):
    hi = x.astype(BF16)
    lo = (x - hi.astype(F32)).astype(BF16)
    return hi, lo


def dot(a, b, dims):
    return lax.dot_general(a, b, dims, preferred_element_type=F32)


def dot3s(a, b, dims):
    (ah, al), (bh, bl) = a, b
    return dot(ah, bh, dims) + (dot(ah, bl, dims) + dot(al, bh, dims))


def dot3(a, b, dims):
    return dot3s(split(a), split(b), dims)


def dot6(a, b, dims):
    return lax.dot_general(a, b, dims, precision=lax.Precision.HIGHEST, preferred_element_type=F32)


def chunk(k):
    return pl.ds(pl.multiple_of(k * CH, CH), CH)


class Sends:
    def __init__(self, sems):
        self.sems = sems
        self.count = 0
        self.pending = []

    def go(self, src, dst, recv, dev, cond=None):
        copy = pltpu.make_async_remote_copy(
            src_ref=src, dst_ref=dst, send_sem=self.sems.at[self.count], recv_sem=recv, device_id=dev, device_id_type=MESH
        )
        self.count += 1
        self.pending.append((copy, cond))
        when(cond, copy.start)

    def drain(self):
        for copy, cond in self.pending:
            when(cond, copy.wait_send)
        self.pending = []


def when(cond, fn):
    if cond is None:
        fn()
    else:
        pl.when(cond)(fn)


def arrived(ref, recv, cond=None):
    copy = pltpu.make_async_copy(ref, ref, recv)
    when(cond, copy.wait)


def reciprocal(x):
    y = pl.reciprocal(x, approx=True)
    return y * (2.0 - x * y)


def pivot8(step, a):
    tiles = [a[8 * t : 8 * t + 8, :] for t in range(8)]
    sub = lax.broadcasted_iota(jnp.int32, (8, 128), 0)
    full = lambda v: jnp.broadcast_to(v, (8, 128))
    cols = [[full(tile[:, i : i + 1]) for i in range(8)] for tile in tiles]
    e = [[full(cols[0][k][i : i + 1, :]) if k >= i else None for k in range(8)] for i in range(8)]
    rows = [full(tiles[0][i : i + 1, :]) for i in range(8)]
    scaled = []
    for i in range(8):
        inv = reciprocal(e[i][i])
        scaled.append(rows[i] * inv)
        for k in range(i + 1, 8):
            f = e[i][k] * inv
            rows[k] = rows[k] - f * rows[i]
            for n in range(k, 8):
                e[k][n] = e[k][n] - f * e[i][n]
            for t in range(1, 8):
                cols[t][k] = cols[t][k] - cols[t][i] * f
    top = rows[0]
    for i in range(1, 8):
        top = jnp.where(sub == i, rows[i], top)
    new = []
    for t in range(1, 8):
        term = cols[t][0] * scaled[0]
        for i in range(1, 8):
            term = term + cols[t][i] * scaled[i]
        new.append(tiles[t] - term * jnp.where(step + t < 8, 1.0, 0.0).astype(F32))
    return pltpu.roll(jnp.concatenate(new + [top], axis=0), 120, axis=1)


def factor_block(aug, k):
    b = 64
    row = lax.broadcasted_iota(jnp.int32, (b, 2 * b), 0)
    col = lax.broadcasted_iota(jnp.int32, (b, 2 * b), 1)
    here = slice(k * b, (k + 1) * b)
    eye = (row + b == col).astype(F32)
    a = jnp.concatenate([aug[here, here], eye[:, b:]], axis=1)
    a = lax.fori_loop(0, 8, pivot8, a)
    diag = jnp.sum(jnp.where(row + b == col, a, 0.0), axis=1, keepdims=True)
    inverse = (a * lax.rsqrt(diag))[:, :b]
    done = dot6(inverse, aug[here, :], PLAIN)
    aug[here, :] = done
    if k < 3:
        below = slice((k + 1) * b, NB)
        aug[below, :] = aug[below, :] - dot6(done[:, (k + 1) * b : NB], done, FIRST)


def exchange_kernel(
    s_hbm, left, right, rfac,
    pr, pc, wr, wc, gf, cf, s, wp, r1, t, r2, u, r3, gp, grs, c0, c1, cy, cz, aug, ac,
    load_sem, send_sem, gsend, gdsend, gasend,
    pr_sem, pc_sem, wr_sem, wc_sem, r1_sem, r2_sem, r3_sem, grs_sem, gf_sem, cy_sem, cz_sem, cf_sem,
):
    p = lax.axis_index("row")
    q = lax.axis_index("col")
    zh, x, c = p // 8, (p // 2) % 4, p % 2
    zl, y = q // 4, q % 4
    same = p == q
    j = x * 2 + c

    load = pltpu.make_async_copy(s_hbm, s, load_sem)
    load.start()

    barrier = pltpu.get_barrier_semaphore()

    def hello(dev):
        pl.semaphore_signal(barrier, inc=1, device_id=dev, device_id_type=MESH)

    def greet(i, carry):
        hello((lax.rem(p + i, 16), q))
        hello((p, lax.rem(q + i, 16)))
        return carry

    lax.fori_loop(1, 16, greet, 0)
    pl.semaphore_wait(barrier, 30)
    load.wait()
    out = Sends(send_sem)

    def send_chunk(buf, sems, k, dev, cond=None):
        out.go(buf.at[chunk(k)], buf.at[chunk(k)], sems.at[k], dev, cond)

    def wait_chunk(buf, sems, k, cond=None):
        arrived(buf.at[chunk(k)], sems.at[k], cond)


    def col_of(i, n):
        return lax.rem(zl + i, 4) * 4 + lax.rem(y + n, 4)

    def col_z(buf, sems, root):
        for i in (1, 3, 2):
            d = col_of(i, 0)
            send_chunk(buf, sems, q, (p, d), (d != 0) if root else None)

    def col_y(buf, sems, root, i):
        k = col_of(i, 0)
        if i:
            wait_chunk(buf, sems, k, (q != 0) if root else None)
        for n in (1, 3, 2):
            d = col_of(0, n)
            send_chunk(buf, sems, k, (p, d), (d != 0) if root else None)

    def col_finish(buf, sems, root):
        for i in (0, 1, 3, 2):
            for n in (1, 3, 2):
                wait_chunk(buf, sems, col_of(i, n), (q != 0) if root else None)


    def pair_send(buf, sems, k, d, cond):
        view = buf.reshape(2, 8, CH, N)
        out.go(view.at[:, k], view.at[:, k], sems.at[k], (d, q), cond)

    def pair_wait(buf, sems, k, cond):
        arrived(buf.reshape(2, 8, CH, N).at[:, k], sems.at[k], cond)

    def pair_spread(buf, sems, here):
        for i in (1, 3, 2):
            d = zh * 8 + lax.rem(x + i, 4) * 2 + c
            pair_send(buf, sems, j, d, here & (d != 0))
        d = zh * 8 + x * 2 + 1 - c
        pair_send(buf, sems, j, d, here & (d != 0))

    def pair_forward(buf, sems, root):
        d = zh * 8 + x * 2 + 1 - c
        for i in (1, 3, 2):
            k = lax.rem(x + i, 4) * 2 + c
            pair_wait(buf, sems, k, (p != 0) if root else None)
            pair_send(buf, sems, k, d, (d != 0) if root else None)

    def pair_finish(buf, sems, root):
        for i in (0, 1, 3, 2):
            pair_wait(buf, sems, lax.rem(x + i, 4) * 2 + 1 - c, (p != 0) if root else None)


    def row_of(z, i, core):
        return z * 8 + lax.rem(x + i, 4) * 2 + core

    def row_spread(buf, sems, k):
        for i in (1, 3, 2):
            send_chunk(buf, sems, k, (row_of(zh, i, c), q))
        send_chunk(buf, sems, k, (row_of(zh, 0, 1 - c), q))

    def row_start(buf, sems):
        send_chunk(buf, sems, p, (row_of(1 - zh, 0, c), q))
        row_spread(buf, sems, p)

    def row_partner(buf, sems):
        k = row_of(1 - zh, 0, c)
        wait_chunk(buf, sems, k)
        row_spread(buf, sems, k)

    def row_own(buf, sems, z):
        for i in (1, 3, 2):
            k = row_of(z, i, c)
            wait_chunk(buf, sems, k)
            send_chunk(buf, sems, k, (row_of(zh, 0, 1 - c), q))

    def row_finish(buf, sems):
        for z in (zh, 1 - zh):
            for i in (0, 1, 3, 2):
                wait_chunk(buf, sems, row_of(z, i, 1 - c))


    def direct(src, dst, ssem, rsem, dev):
        return pltpu.make_async_remote_copy(
            src_ref=src, dst_ref=dst, send_sem=ssem, recv_sem=rsem, device_id=dev, device_id_type=MESH
        )

    def gram_copy(i):
        d = lax.rem(q + i, 16)
        return direct(gp.at[chunk(d)], grs.at[q], gsend.at[i], grs_sem.at[q], (p, d))

    def gram_all(i):
        d = lax.rem(q + i, 16)
        return direct(gf.at[chunk(q)], gf.at[chunk(q)], gasend.at[i], gf_sem.at[q], (p, d))

    def gram_down(i):
        return direct(gf.at[chunk(q)], gf.at[chunk(q)], gdsend.at[i], gf_sem.at[q], (i, q))

    def start_all(make):
        lax.fori_loop(1, 16, lambda i, z: (make(i).start(), z)[1], 0)

    def drain_all(make):
        lax.fori_loop(1, 16, lambda i, z: (make(i).wait_send(), z)[1], 0)

    def wait_slots(buf, sems, me):
        def step(i, z):
            k = lax.rem(me + i, 16)
            arrived(buf.at[k], sems.at[k])
            return z

        lax.fori_loop(1, 16, step, 0)

    def wait_chunks(buf, sems, me):
        def step(i, z):
            wait_chunk(buf, sems, lax.rem(me + i, 16))
            return z

        lax.fori_loop(1, 16, step, 0)

    lane = lax.broadcasted_iota(jnp.int32, (NB, N), 1)

    @pl.when(p == 0)
    def _():
        pc[...] = jnp.where((q == 0) & (lane < NB), 0.0, s[0:NB, :])

    for k in (4, 5, 2, 3, 6, 7, 1):
        pair_send(pc, pc_sem, k, k, p == 0)

    @pl.when(p == 0)
    def _():
        both = split(pc[...])
        gp[...] = dot3s(both, both, LAST)
        grs[pl.ds(q, 1)] = gp[chunk(q), :][None]
        start_all(gram_copy)

    @pl.when(q == 0)
    def _():
        pr[...] = jnp.where((p == 0) & (lane < NB), 0.0, s[:, 0:NB].T)

    for i in range(4):
        for n in (1, 3, 2):
            send_chunk(pr, pr_sem, i * 4 + n, (p, n), q == 0)

    def line(i, here):
        k = i * 4 + y
        wait_chunk(pr, pr_sem, k, here & (q != 0))
        send_chunk(pr, pr_sem, k, (p, lax.rem(q + 4, 16)), here & (zl < 3))
        for n in (1, 3, 2):
            d = col_of(0, n)
            send_chunk(pr, pr_sem, k, (p, d), here & (d != 0))

    near, far, first = zh == 0, zh == 1, zl == 0
    line(0, first)
    pair_wait(pc, pc_sem, j, near & (p != 0))
    pair_send(pc, pc_sem, j, 8 + j, near)
    pair_spread(pc, pc_sem, near)
    line(0, zl > 0)
    line(1, zl >= 0)

    @pl.when(p == 0)
    def _():
        wait_slots(grs, grs_sem, q)
        gf[chunk(q), :] = jnp.sum(grs[...], axis=0)
        start_all(gram_down)

    line(2, zl >= 0)
    pair_wait(pc, pc_sem, j, far)
    pair_spread(pc, pc_sem, far)
    line(3, zl >= 0)
    pair_forward(pc, pc_sem, True)
    pair_finish(pc, pc_sem, True)
    wait_chunk(gf, gf_sem, q, p != 0)
    start_all(gram_all)

    col_finish(pr, pr_sem, True)
    prh, prl = split(pr[...])

    def product(i, z):
        cols = pl.ds(pl.multiple_of(i * 256, 256), 256)
        wp.reshape(NB, N)[:, cols] = dot3s((prh, prl), split(s[:, cols]), PLAIN)
        return z

    lax.fori_loop(0, 4, product, 0)

    out.go(wp.at[:, 1 - c], r1, r1_sem, (zh * 8 + x * 2 + 1 - c, q))
    arrived(r1, r1_sem)
    t[...] = wp[:, pl.ds(c, 1)][:, 0] + r1[...]
    for phase, z in ((0, 1 - zh), (1, zh)):
        for i in (1, 3, 2):
            xx = lax.rem(x + i, 4)
            out.go(t.at[z * 4 + xx], r2.at[phase, i - 1], r2_sem.at[phase, i - 1], (zh * 8 + xx * 2 + c, q))
    wait_chunks(gf, gf_sem, q)
    row = lax.broadcasted_iota(jnp.int32, (NB, NB), 0)
    col = lax.broadcasted_iota(jnp.int32, (NB, NB), 1)
    aug[:, 0:NB] = gf[...]
    aug[:, NB:] = (row == col).astype(F32)
    factor_block(aug, 0)
    for i in (1, 3, 2):
        arrived(r2.at[0, i - 1], r2_sem.at[0, i - 1])
    u[...] = t[(1 - zh) * 4 + x] + (r2[0, 0] + r2[0, 1] + r2[0, 2])
    out.go(u, r3, r3_sem, ((1 - zh) * 8 + j, q))
    factor_block(aug, 1)
    for i in (1, 3, 2):
        arrived(r2.at[1, i - 1], r2_sem.at[1, i - 1])
    part = t[zh * 4 + x] + (r2[1, 0] + r2[1, 1] + r2[1, 2])
    arrived(r3, r3_sem)
    mine = part + r3[...]
    wc[chunk(p), :] = mine

    curv = cf.reshape(2, 4, 2, CH, NB)
    c0[...] = dot3(mine, pc[...], LAST)
    for i in (1, 3, 2):
        out.go(c0, cy.at[i - 1], cy_sem.at[i - 1], (p, col_of(0, i)))
    out.go(wc.at[chunk(p)], wr.at[chunk(p)], wr_sem.at[p], (q, p), p != q)
    row_start(wc, wc_sem)

    @pl.when(same)
    def _():
        wr[chunk(q), :] = mine

    factor_block(aug, 2)
    for i in (1, 3, 2):
        arrived(cy.at[i - 1], cy_sem.at[i - 1])
    c1[...] = c0[...] + (cy[0] + cy[1] + cy[2])
    for i in (1, 3, 2):
        out.go(c1, cz.at[i - 1], cz_sem.at[i - 1], (p, col_of(i, 0)))
    factor_block(aug, 3)
    wait_chunk(wr, wr_sem, q, p != q)
    col_z(wr, wr_sem, False)
    col_y(wr, wr_sem, False, 0)
    for i in (1, 3, 2):
        arrived(cz.at[i - 1], cz_sem.at[i - 1])
    cf[chunk(p), :] = c1[...] + (cz[0] + cz[1] + cz[2])
    out.go(cf.at[chunk(p)], cf.at[chunk(p)], cf_sem.at[0], (row_of(1 - zh, 0, c), q))
    row_partner(wc, wc_sem)
    rfac[...] = jnp.where(row <= col, aug[:, 0:NB], 0.0)
    inverse = aug[:, NB:]
    m = split(2.0 * dot6(inverse, inverse, FIRST))
    ac[...] = dot3s(m, split(pc[...]), PLAIN)
    ah, al = split(ac[...])
    right[NB : 2 * NB, :] = ah
    right[3 * NB : 4 * NB, :] = al
    for i in (1, 3, 2):
        col_y(wr, wr_sem, False, i)
    arrived(cf.at[chunk(row_of(1 - zh, 0, c))], cf_sem.at[0])
    for i in (1, 3, 2):
        out.go(curv.at[:, x, c], curv.at[:, x, c], cf_sem.at[i], (row_of(zh, i, c), q))
    row_own(wc, wc_sem, zh)
    rh, rl = split(dot3s(m, split(pr[...]), PLAIN).T)
    left[:, 0:NB] = rh
    left[:, 2 * NB : 3 * NB] = rl
    for i in (1, 3, 2):
        arrived(curv.at[:, lax.rem(x + 4 - i, 4), c], cf_sem.at[i])
    out.go(curv.at[:, :, c], curv.at[:, :, c], cf_sem.at[4], (row_of(zh, 0, 1 - c), q))
    row_own(wc, wc_sem, 1 - zh)
    arrived(curv.at[:, :, 1 - c], cf_sem.at[4])

    turned = dot3s(split(cf[...]), (ah, al), PLAIN)
    row_finish(wc, wc_sem)
    vh, vl = split(wc[...] - turned)
    right[0:NB, :] = vh
    right[2 * NB : 3 * NB, :] = vl
    col_finish(wr, wr_sem, False)
    vh, vl = split(wr[...].T)
    left[:, NB : 2 * NB] = vh
    left[:, 3 * NB : 4 * NB] = vl
    out.drain()

    @pl.when(p == 0)
    def _():
        drain_all(gram_copy)
        drain_all(gram_down)

    drain_all(gram_all)


def exchange(matrix):
    vm = pl.BlockSpec(memory_space=pltpu.VMEM)
    dma = pltpu.SemaphoreType.DMA
    big = pltpu.VMEM((NB, N), F32)
    small = pltpu.VMEM((NB, NB), F32)
    return pl.pallas_call(
        exchange_kernel,
        out_shape=(
            jax.ShapeDtypeStruct((N, 4 * NB), BF16),
            jax.ShapeDtypeStruct((4 * NB, N), BF16),
            jax.ShapeDtypeStruct((NB, NB), F32),
        ),
        in_specs=[pl.BlockSpec(memory_space=pltpu.HBM)],
        out_specs=(vm,) * 3,
        scratch_shapes=[
            big, big, big, big, small, small,
            pltpu.VMEM((N, N), F32),
            pltpu.VMEM((8, 2, CH, N), F32),
            pltpu.VMEM((8, CH, N), F32),
            pltpu.VMEM((8, CH, N), F32),
            pltpu.VMEM((2, 3, CH, N), F32),
            pltpu.VMEM((CH, N), F32),
            pltpu.VMEM((CH, N), F32),
            small,
            pltpu.VMEM((16, CH, NB), F32),
            pltpu.VMEM((CH, NB), F32),
            pltpu.VMEM((CH, NB), F32),
            pltpu.VMEM((3, CH, NB), F32),
            pltpu.VMEM((3, CH, NB), F32),
            pltpu.VMEM((NB, 2 * NB), F32),
            big,
            dma, dma((112,)), dma((16,)), dma((16,)), dma((16,)),
            dma((16,)), dma((8,)), dma((16,)), dma((16,)), dma, dma((2, 3)), dma,
            dma((16,)), dma((16,)), dma((3,)), dma((3,)), dma((5,)),
        ],
        compiler_params=pltpu.CompilerParams(collective_id=0, has_side_effects=True, vmem_limit_bytes=48 << 20),
        name="exchange",
    )(matrix)


TILE = 128


def finish_kernel(left, right, factor, s, out, r, buf, sems, r_sem):
    r_copy = pltpu.make_async_copy(factor, r, r_sem)
    r_copy.start()
    half = 2 * NB
    copies = []
    for i in range(N // TILE):
        rows = slice(i * TILE, (i + 1) * TILE)
        lh, ll = left[rows, 0:half], left[rows, half:]
        rh, rl = right[0:half, :], right[half:, :]
        buf[rows, :] = s[rows, :] - (dot(lh, rh, PLAIN) + (dot(lh, rl, PLAIN) + dot(ll, rh, PLAIN)))
        copies.append(pltpu.make_async_copy(buf.at[rows], out.at[rows], sems.at[i]))
        copies[-1].start()
    for copy in copies:
        copy.wait()
    r_copy.wait()


def finish(left, right, factor, matrix):
    vm, anywhere = pl.BlockSpec(memory_space=pltpu.VMEM), pl.BlockSpec(memory_space=pl.ANY)
    dma = pltpu.SemaphoreType.DMA
    return pl.pallas_call(
        finish_kernel,
        out_shape=(jax.ShapeDtypeStruct((N, N), F32), jax.ShapeDtypeStruct((NB, NB), F32)),
        in_specs=[vm] * 4,
        out_specs=(anywhere, anywhere),
        scratch_shapes=[pltpu.VMEM((N, N), F32), dma((N // TILE,)), dma],
        compiler_params=pltpu.CompilerParams(vmem_limit_bytes=32 << 20),
        name="finish",
    )(left, right, factor, matrix)


def on_device(matrix):
    return finish(*exchange(matrix), matrix)


def solution(mesh):
    return jax.shard_map(
        on_device,
        mesh=mesh,
        in_specs=(P("row", "col"),),
        out_specs=(P("row", "col"), P()),
        check_vma=False,
    )
```

```python
import functools
import jax
import jax.numpy as jnp
from jax import lax
from jax.experimental import pallas as pl
from jax.experimental.pallas import tpu as pltpu
from jax.sharding import PartitionSpec as P

NB = 256
N = 1024
CH = 16
MESH = pl.DeviceIdType.MESH
F32 = jnp.float32
BF16 = jnp.bfloat16

LAST = (((1,), (1,)), ((), ()))
FIRST = (((0,), (0,)), ((), ()))
PLAIN = (((1,), (0,)), ((), ()))


def split(x):
    hi = x.astype(BF16)
    lo = (x - hi.astype(F32)).astype(BF16)
    return hi, lo


def dot(a, b, dims):
    return lax.dot_general(a, b, dims, preferred_element_type=F32)


def dot3s(a, b, dims):
    (ah, al), (bh, bl) = a, b
    return dot(ah, bh, dims) + (dot(ah, bl, dims) + dot(al, bh, dims))


def dot3(a, b, dims):
    return dot3s(split(a), split(b), dims)


def dot6(a, b, dims):
    return lax.dot_general(a, b, dims, precision=lax.Precision.HIGHEST, preferred_element_type=F32)


def chunk(k):
    return pl.ds(pl.multiple_of(k * CH, CH), CH)


class Sends:
    def __init__(self, sems):
        self.sems = sems
        self.count = 0
        self.pending = []

    def go(self, src, dst, recv, dev, cond=None):
        copy = pltpu.make_async_remote_copy(
            src_ref=src, dst_ref=dst, send_sem=self.sems.at[self.count], recv_sem=recv, device_id=dev, device_id_type=MESH
        )
        self.count += 1
        self.pending.append((copy, cond))
        when(cond, copy.start)

    def drain(self):
        for copy, cond in self.pending:
            when(cond, copy.wait_send)
        self.pending = []


def when(cond, fn):
    if cond is None:
        fn()
    else:
        pl.when(cond)(fn)


def arrived(ref, recv, cond=None):
    copy = pltpu.make_async_copy(ref, ref, recv)
    when(cond, copy.wait)


def reciprocal(x):
    y = pl.reciprocal(x, approx=True)
    return y * (2.0 - x * y)


def pivot8(step, a):
    tiles = [a[8 * t : 8 * t + 8, :] for t in range(8)]
    sub = lax.broadcasted_iota(jnp.int32, (8, 128), 0)
    full = lambda v: jnp.broadcast_to(v, (8, 128))
    cols = [[full(tile[:, i : i + 1]) for i in range(8)] for tile in tiles]
    e = [[full(cols[0][k][i : i + 1, :]) if k >= i else None for k in range(8)] for i in range(8)]
    rows = [full(tiles[0][i : i + 1, :]) for i in range(8)]
    scaled = []
    for i in range(8):
        inv = reciprocal(e[i][i])
        scaled.append(rows[i] * inv)
        for k in range(i + 1, 8):
            f = e[i][k] * inv
            rows[k] = rows[k] - f * rows[i]
            for n in range(k, 8):
                e[k][n] = e[k][n] - f * e[i][n]
            for t in range(1, 8):
                cols[t][k] = cols[t][k] - cols[t][i] * f
    top = rows[0]
    for i in range(1, 8):
        top = jnp.where(sub == i, rows[i], top)
    new = []
    for t in range(1, 8):
        term = cols[t][0] * scaled[0]
        for i in range(1, 8):
            term = term + cols[t][i] * scaled[i]
        new.append(tiles[t] - term * jnp.where(step + t < 8, 1.0, 0.0).astype(F32))
    return pltpu.roll(jnp.concatenate(new + [top], axis=0), 120, axis=1)


def factor_block(aug, k):
    b = 64
    row = lax.broadcasted_iota(jnp.int32, (b, 2 * b), 0)
    col = lax.broadcasted_iota(jnp.int32, (b, 2 * b), 1)
    here = slice(k * b, (k + 1) * b)
    eye = (row + b == col).astype(F32)
    a = jnp.concatenate([aug[here, here], eye[:, b:]], axis=1)
    a = lax.fori_loop(0, 8, pivot8, a)
    diag = jnp.sum(jnp.where(row + b == col, a, 0.0), axis=1, keepdims=True)
    inverse = (a * lax.rsqrt(diag))[:, :b]
    done = dot6(inverse, aug[here, :], PLAIN)
    aug[here, :] = done
    if k < 3:
        below = slice((k + 1) * b, NB)
        aug[below, :] = aug[below, :] - dot6(done[:, (k + 1) * b : NB], done, FIRST)


def exchange_kernel(
    s_hbm, left, right, rfac,
    pr, pc, wr, wc, gf, cf, s, wp, r1, t, r2, u, r3, gp, grs, c0, c1, cy, cz, aug, ac,
    load_sem, send_sem, gsend, gdsend, gasend,
    pr_sem, pc_sem, wr_sem, wc_sem, r1_sem, r2_sem, r3_sem, grs_sem, gf_sem, cy_sem, cz_sem, cf_sem,
):
    p = lax.axis_index("row")
    q = lax.axis_index("col")
    zh, x, c = p // 8, (p // 2) % 4, p % 2
    zl, y = q // 4, q % 4
    same = p == q
    j = x * 2 + c

    load = pltpu.make_async_copy(s_hbm, s, load_sem)
    load.start()

    barrier = pltpu.get_barrier_semaphore()

    def hello(dev):
        pl.semaphore_signal(barrier, inc=1, device_id=dev, device_id_type=MESH)

    def greet(i, carry):
        hello((lax.rem(p + i, 16), q))
        hello((p, lax.rem(q + i, 16)))
        return carry

    lax.fori_loop(1, 16, greet, 0)
    pl.semaphore_wait(barrier, 30)
    load.wait()
    out = Sends(send_sem)

    def send_chunk(buf, sems, k, dev, cond=None):
        out.go(buf.at[chunk(k)], buf.at[chunk(k)], sems.at[k], dev, cond)

    def wait_chunk(buf, sems, k, cond=None):
        arrived(buf.at[chunk(k)], sems.at[k], cond)


    def col_of(i, n):
        return lax.rem(zl + i, 4) * 4 + lax.rem(y + n, 4)

    def col_z(buf, sems, root):
        for i in (1, 3, 2):
            d = col_of(i, 0)
            send_chunk(buf, sems, q, (p, d), (d != 0) if root else None)

    def col_y(buf, sems, root, i):
        k = col_of(i, 0)
        if i:
            wait_chunk(buf, sems, k, (q != 0) if root else None)
        for n in (2, 1, 3):
            d = col_of(0, n)
            send_chunk(buf, sems, k, (p, d), (d != 0) if root else None)

    def col_finish(buf, sems, root):
        for i in (0, 1, 3, 2):
            for n in (1, 3, 2):
                wait_chunk(buf, sems, col_of(i, n), (q != 0) if root else None)


    def pair_send(buf, sems, k, d, cond):
        view = buf.reshape(2, 8, CH, N)
        out.go(view.at[:, k], view.at[:, k], sems.at[k], (d, q), cond)

    def pair_wait(buf, sems, k, cond):
        arrived(buf.reshape(2, 8, CH, N).at[:, k], sems.at[k], cond)

    def pair_spread(buf, sems, here):
        for i in (1, 3, 2):
            d = zh * 8 + lax.rem(x + i, 4) * 2 + c
            pair_send(buf, sems, j, d, here & (d != 0))
        d = zh * 8 + x * 2 + 1 - c
        pair_send(buf, sems, j, d, here & (d != 0))

    def pair_forward(buf, sems, root):
        d = zh * 8 + x * 2 + 1 - c
        for i in (1, 3, 2):
            k = lax.rem(x + i, 4) * 2 + c
            pair_wait(buf, sems, k, (p != 0) if root else None)
            pair_send(buf, sems, k, d, (d != 0) if root else None)

    def pair_finish(buf, sems, root):
        for i in (0, 1, 3, 2):
            pair_wait(buf, sems, lax.rem(x + i, 4) * 2 + 1 - c, (p != 0) if root else None)


    def row_of(z, i, core):
        return z * 8 + lax.rem(x + i, 4) * 2 + core

    def row_spread(buf, sems, k):
        for i in (1, 3, 2):
            send_chunk(buf, sems, k, (row_of(zh, i, c), q))
        send_chunk(buf, sems, k, (row_of(zh, 0, 1 - c), q))

    def row_start(buf, sems):
        send_chunk(buf, sems, p, (row_of(1 - zh, 0, c), q))
        row_spread(buf, sems, p)

    def row_partner(buf, sems):
        k = row_of(1 - zh, 0, c)
        wait_chunk(buf, sems, k)
        row_spread(buf, sems, k)

    def row_own(buf, sems, z):
        for i in (1, 3, 2):
            k = row_of(z, i, c)
            wait_chunk(buf, sems, k)
            send_chunk(buf, sems, k, (row_of(zh, 0, 1 - c), q))

    def row_finish(buf, sems):
        for z in (zh, 1 - zh):
            for i in (0, 1, 3, 2):
                wait_chunk(buf, sems, row_of(z, i, 1 - c))


    def direct(src, dst, ssem, rsem, dev):
        return pltpu.make_async_remote_copy(
            src_ref=src, dst_ref=dst, send_sem=ssem, recv_sem=rsem, device_id=dev, device_id_type=MESH
        )

    def gram_copy(i):
        d = lax.rem(q + i, 16)
        return direct(gp.at[chunk(d)], grs.at[q], gsend.at[i], grs_sem.at[q], (p, d))

    def gram_all(i):
        d = lax.rem(q + i, 16)
        return direct(gf.at[chunk(q)], gf.at[chunk(q)], gasend.at[i], gf_sem.at[q], (p, d))

    def gram_down(i):
        return direct(gf.at[chunk(q)], gf.at[chunk(q)], gdsend.at[i], gf_sem.at[q], (i, q))

    def start_all(make):
        lax.fori_loop(1, 16, lambda i, z: (make(i).start(), z)[1], 0)

    def drain_all(make):
        lax.fori_loop(1, 16, lambda i, z: (make(i).wait_send(), z)[1], 0)

    def wait_slots(buf, sems, me):
        def step(i, z):
            k = lax.rem(me + i, 16)
            arrived(buf.at[k], sems.at[k])
            return z

        lax.fori_loop(1, 16, step, 0)

    def wait_chunks(buf, sems, me):
        def step(i, z):
            wait_chunk(buf, sems, lax.rem(me + i, 16))
            return z

        lax.fori_loop(1, 16, step, 0)

    lane = lax.broadcasted_iota(jnp.int32, (NB, N), 1)

    @pl.when(p == 0)
    def _():
        pc[...] = jnp.where((q == 0) & (lane < NB), 0.0, s[0:NB, :])

    for k in (4, 5, 2, 3, 6, 7, 1):
        pair_send(pc, pc_sem, k, k, p == 0)

    @pl.when(p == 0)
    def _():
        both = split(pc[...])
        gp[...] = dot3s(both, both, LAST)
        grs[pl.ds(q, 1)] = gp[chunk(q), :][None]
        start_all(gram_copy)

    @pl.when(q == 0)
    def _():
        pr[...] = jnp.where((p == 0) & (lane < NB), 0.0, s[:, 0:NB].T)

    for i in range(4):
        for n in (1, 3, 2):
            send_chunk(pr, pr_sem, i * 4 + n, (p, n), q == 0)

    def line(i, here):
        k = i * 4 + y
        wait_chunk(pr, pr_sem, k, here & (q != 0))
        send_chunk(pr, pr_sem, k, (p, lax.rem(q + 4, 16)), here & (zl < 3))
        for n in (2, 1, 3):
            d = col_of(0, n)
            send_chunk(pr, pr_sem, k, (p, d), here & (d != 0))

    near, far, first = zh == 0, zh == 1, zl == 0
    line(0, first)
    pair_wait(pc, pc_sem, j, near & (p != 0))
    pair_send(pc, pc_sem, j, 8 + j, near)
    pair_spread(pc, pc_sem, near)
    line(0, zl > 0)
    line(1, zl >= 0)

    @pl.when(p == 0)
    def _():
        wait_slots(grs, grs_sem, q)
        gf[chunk(q), :] = jnp.sum(grs[...], axis=0)
        start_all(gram_down)

    line(2, zl >= 0)
    pair_wait(pc, pc_sem, j, far)
    pair_spread(pc, pc_sem, far)
    line(3, zl >= 0)
    pair_forward(pc, pc_sem, True)
    pair_finish(pc, pc_sem, True)
    wait_chunk(gf, gf_sem, q, p != 0)
    start_all(gram_all)

    col_finish(pr, pr_sem, True)
    prh, prl = split(pr[...])

    def product(i, z):
        cols = pl.ds(pl.multiple_of(i * 256, 256), 256)
        wp.reshape(NB, N)[:, cols] = dot3s((prh, prl), split(s[:, cols]), PLAIN)
        return z

    lax.fori_loop(0, 4, product, 0)

    out.go(wp.at[:, 1 - c], r1, r1_sem, (zh * 8 + x * 2 + 1 - c, q))
    arrived(r1, r1_sem)
    t[...] = wp[:, pl.ds(c, 1)][:, 0] + r1[...]
    for phase, z in ((0, 1 - zh), (1, zh)):
        for i in (1, 3, 2):
            xx = lax.rem(x + i, 4)
            out.go(t.at[z * 4 + xx], r2.at[phase, i - 1], r2_sem.at[phase, i - 1], (zh * 8 + xx * 2 + c, q))
    wait_chunks(gf, gf_sem, q)
    row = lax.broadcasted_iota(jnp.int32, (NB, NB), 0)
    col = lax.broadcasted_iota(jnp.int32, (NB, NB), 1)
    aug[:, 0:NB] = gf[...]
    aug[:, NB:] = (row == col).astype(F32)
    factor_block(aug, 0)
    for i in (1, 3, 2):
        arrived(r2.at[0, i - 1], r2_sem.at[0, i - 1])
    u[...] = t[(1 - zh) * 4 + x] + (r2[0, 0] + r2[0, 1] + r2[0, 2])
    out.go(u, r3, r3_sem, ((1 - zh) * 8 + j, q))
    factor_block(aug, 1)
    for i in (1, 3, 2):
        arrived(r2.at[1, i - 1], r2_sem.at[1, i - 1])
    part = t[zh * 4 + x] + (r2[1, 0] + r2[1, 1] + r2[1, 2])
    arrived(r3, r3_sem)
    mine = part + r3[...]
    wc[chunk(p), :] = mine

    curv = cf.reshape(2, 4, 2, CH, NB)
    c0[...] = dot3(mine, pc[...], LAST)
    for i in (1, 3, 2):
        out.go(c0, cy.at[i - 1], cy_sem.at[i - 1], (p, col_of(0, i)))
    out.go(wc.at[chunk(p)], wr.at[chunk(p)], wr_sem.at[p], (q, p), p != q)
    row_start(wc, wc_sem)

    @pl.when(same)
    def _():
        wr[chunk(q), :] = mine

    factor_block(aug, 2)
    for i in (1, 3, 2):
        arrived(cy.at[i - 1], cy_sem.at[i - 1])
    c1[...] = c0[...] + (cy[0] + cy[1] + cy[2])
    for i in (1, 3, 2):
        out.go(c1, cz.at[i - 1], cz_sem.at[i - 1], (p, col_of(i, 0)))
    wait_chunk(wr, wr_sem, q, p != q)
    col_z(wr, wr_sem, False)
    col_y(wr, wr_sem, False, 0)
    factor_block(aug, 3)
    for i in (1, 3, 2):
        arrived(cz.at[i - 1], cz_sem.at[i - 1])
    cf[chunk(p), :] = c1[...] + (cz[0] + cz[1] + cz[2])
    out.go(cf.at[chunk(p)], cf.at[chunk(p)], cf_sem.at[0], (row_of(1 - zh, 0, c), q))
    row_partner(wc, wc_sem)
    rfac[...] = jnp.where(row <= col, aug[:, 0:NB], 0.0)
    inverse = aug[:, NB:]
    m = split(2.0 * dot6(inverse, inverse, FIRST))
    ac[...] = dot3s(m, split(pc[...]), PLAIN)
    ah, al = split(ac[...])
    right[NB : 2 * NB, :] = ah
    right[3 * NB : 4 * NB, :] = al
    for i in (1, 3, 2):
        col_y(wr, wr_sem, False, i)
    arrived(cf.at[chunk(row_of(1 - zh, 0, c))], cf_sem.at[0])
    for i in (1, 3, 2):
        out.go(curv.at[:, x, c], curv.at[:, x, c], cf_sem.at[i], (row_of(zh, i, c), q))
    row_own(wc, wc_sem, zh)
    rh, rl = split(dot3s(m, split(pr[...]), PLAIN).T)
    left[:, 0:NB] = rh
    left[:, 2 * NB : 3 * NB] = rl
    for i in (1, 3, 2):
        arrived(curv.at[:, lax.rem(x + 4 - i, 4), c], cf_sem.at[i])
    out.go(curv.at[:, :, c], curv.at[:, :, c], cf_sem.at[4], (row_of(zh, 0, 1 - c), q))
    row_own(wc, wc_sem, 1 - zh)
    arrived(curv.at[:, :, 1 - c], cf_sem.at[4])

    turned = dot3s(split(cf[...]), (ah, al), PLAIN)
    row_finish(wc, wc_sem)
    vh, vl = split(wc[...] - turned)
    right[0:NB, :] = vh
    right[2 * NB : 3 * NB, :] = vl
    col_finish(wr, wr_sem, False)
    vh, vl = split(wr[...].T)
    left[:, NB : 2 * NB] = vh
    left[:, 3 * NB : 4 * NB] = vl
    out.drain()

    @pl.when(p == 0)
    def _():
        drain_all(gram_copy)
        drain_all(gram_down)

    drain_all(gram_all)


def exchange(matrix):
    vm = pl.BlockSpec(memory_space=pltpu.VMEM)
    dma = pltpu.SemaphoreType.DMA
    big = pltpu.VMEM((NB, N), F32)
    small = pltpu.VMEM((NB, NB), F32)
    return pl.pallas_call(
        exchange_kernel,
        out_shape=(
            jax.ShapeDtypeStruct((N, 4 * NB), BF16),
            jax.ShapeDtypeStruct((4 * NB, N), BF16),
            jax.ShapeDtypeStruct((NB, NB), F32),
        ),
        in_specs=[pl.BlockSpec(memory_space=pltpu.HBM)],
        out_specs=(vm,) * 3,
        scratch_shapes=[
            big, big, big, big, small, small,
            pltpu.VMEM((N, N), F32),
            pltpu.VMEM((8, 2, CH, N), F32),
            pltpu.VMEM((8, CH, N), F32),
            pltpu.VMEM((8, CH, N), F32),
            pltpu.VMEM((2, 3, CH, N), F32),
            pltpu.VMEM((CH, N), F32),
            pltpu.VMEM((CH, N), F32),
            small,
            pltpu.VMEM((16, CH, NB), F32),
            pltpu.VMEM((CH, NB), F32),
            pltpu.VMEM((CH, NB), F32),
            pltpu.VMEM((3, CH, NB), F32),
            pltpu.VMEM((3, CH, NB), F32),
            pltpu.VMEM((NB, 2 * NB), F32),
            big,
            dma, dma((112,)), dma((16,)), dma((16,)), dma((16,)),
            dma((16,)), dma((8,)), dma((16,)), dma((16,)), dma, dma((2, 3)), dma,
            dma((16,)), dma((16,)), dma((3,)), dma((3,)), dma((5,)),
        ],
        compiler_params=pltpu.CompilerParams(collective_id=0, has_side_effects=True, vmem_limit_bytes=48 << 20),
        name="exchange",
    )(matrix)


TILE = 128


def finish_kernel(left, right, factor, s, out, r, buf, sems, r_sem):
    r_copy = pltpu.make_async_copy(factor, r, r_sem)
    r_copy.start()
    half = 2 * NB
    copies = []
    for i in range(N // TILE):
        rows = slice(i * TILE, (i + 1) * TILE)
        lh, ll = left[rows, 0:half], left[rows, half:]
        rh, rl = right[0:half, :], right[half:, :]
        buf[rows, :] = s[rows, :] - (dot(lh, rh, PLAIN) + (dot(lh, rl, PLAIN) + dot(ll, rh, PLAIN)))
        copies.append(pltpu.make_async_copy(buf.at[rows], out.at[rows], sems.at[i]))
        copies[-1].start()
    for copy in copies:
        copy.wait()
    r_copy.wait()


def finish(left, right, factor, matrix):
    vm, anywhere = pl.BlockSpec(memory_space=pltpu.VMEM), pl.BlockSpec(memory_space=pl.ANY)
    dma = pltpu.SemaphoreType.DMA
    return pl.pallas_call(
        finish_kernel,
        out_shape=(jax.ShapeDtypeStruct((N, N), F32), jax.ShapeDtypeStruct((NB, NB), F32)),
        in_specs=[vm] * 4,
        out_specs=(anywhere, anywhere),
        scratch_shapes=[pltpu.VMEM((N, N), F32), dma((N // TILE,)), dma],
        compiler_params=pltpu.CompilerParams(vmem_limit_bytes=32 << 20),
        name="finish",
    )(left, right, factor, matrix)


def on_device(matrix):
    return finish(*exchange(matrix), matrix)


def solution(mesh):
    return jax.shard_map(
        on_device,
        mesh=mesh,
        in_specs=(P("row", "col"),),
        out_specs=(P("row", "col"), P()),
        check_vma=False,
    )
```

```python
import functools
import jax
import jax.numpy as jnp
from jax import lax
from jax.experimental import pallas as pl
from jax.experimental.pallas import tpu as pltpu
from jax.sharding import PartitionSpec as P

NB = 256
N = 1024
CH = 16
MESH = pl.DeviceIdType.MESH
F32 = jnp.float32
BF16 = jnp.bfloat16

LAST = (((1,), (1,)), ((), ()))
FIRST = (((0,), (0,)), ((), ()))
PLAIN = (((1,), (0,)), ((), ()))


def split(x):
    hi = x.astype(BF16)
    lo = (x - hi.astype(F32)).astype(BF16)
    return hi, lo


def dot(a, b, dims):
    return lax.dot_general(a, b, dims, preferred_element_type=F32)


def dot3s(a, b, dims):
    (ah, al), (bh, bl) = a, b
    return dot(ah, bh, dims) + (dot(ah, bl, dims) + dot(al, bh, dims))


def dot3(a, b, dims):
    return dot3s(split(a), split(b), dims)


def dot6(a, b, dims):
    return lax.dot_general(a, b, dims, precision=lax.Precision.HIGHEST, preferred_element_type=F32)


def chunk(k):
    return pl.ds(pl.multiple_of(k * CH, CH), CH)


class Sends:
    def __init__(self, sems):
        self.sems = sems
        self.count = 0
        self.pending = []

    def go(self, src, dst, recv, dev, cond=None):
        copy = pltpu.make_async_remote_copy(
            src_ref=src, dst_ref=dst, send_sem=self.sems.at[self.count], recv_sem=recv, device_id=dev, device_id_type=MESH
        )
        self.count += 1
        self.pending.append((copy, cond))
        when(cond, copy.start)

    def drain(self):
        for copy, cond in self.pending:
            when(cond, copy.wait_send)
        self.pending = []


def when(cond, fn):
    if cond is None:
        fn()
    else:
        pl.when(cond)(fn)


def arrived(ref, recv, cond=None):
    copy = pltpu.make_async_copy(ref, ref, recv)
    when(cond, copy.wait)


def reciprocal(x):
    y = pl.reciprocal(x, approx=True)
    return y * (2.0 - x * y)


def pivot8(step, a):
    tiles = [a[8 * t : 8 * t + 8, :] for t in range(8)]
    sub = lax.broadcasted_iota(jnp.int32, (8, 128), 0)
    full = lambda v: jnp.broadcast_to(v, (8, 128))
    cols = [[full(tile[:, i : i + 1]) for i in range(8)] for tile in tiles]
    e = [[full(cols[0][k][i : i + 1, :]) if k >= i else None for k in range(8)] for i in range(8)]
    rows = [full(tiles[0][i : i + 1, :]) for i in range(8)]
    scaled = []
    for i in range(8):
        inv = reciprocal(e[i][i])
        scaled.append(rows[i] * inv)
        for k in range(i + 1, 8):
            f = e[i][k] * inv
            rows[k] = rows[k] - f * rows[i]
            for n in range(k, 8):
                e[k][n] = e[k][n] - f * e[i][n]
            for t in range(1, 8):
                cols[t][k] = cols[t][k] - cols[t][i] * f
    top = rows[0]
    for i in range(1, 8):
        top = jnp.where(sub == i, rows[i], top)
    new = []
    for t in range(1, 8):
        term = cols[t][0] * scaled[0]
        for i in range(1, 8):
            term = term + cols[t][i] * scaled[i]
        new.append(tiles[t] - term * jnp.where(step + t < 8, 1.0, 0.0).astype(F32))
    return pltpu.roll(jnp.concatenate(new + [top], axis=0), 120, axis=1)


def factor_block(aug, k):
    b = 64
    row = lax.broadcasted_iota(jnp.int32, (b, 2 * b), 0)
    col = lax.broadcasted_iota(jnp.int32, (b, 2 * b), 1)
    here = slice(k * b, (k + 1) * b)
    eye = (row + b == col).astype(F32)
    a = jnp.concatenate([aug[here, here], eye[:, b:]], axis=1)
    a = lax.fori_loop(0, 8, pivot8, a)
    diag = jnp.sum(jnp.where(row + b == col, a, 0.0), axis=1, keepdims=True)
    inverse = (a * lax.rsqrt(diag))[:, :b]
    done = dot6(inverse, aug[here, :], PLAIN)
    aug[here, :] = done
    if k < 3:
        below = slice((k + 1) * b, NB)
        aug[below, :] = aug[below, :] - dot6(done[:, (k + 1) * b : NB], done, FIRST)


def exchange_kernel(
    s_hbm, left, right, rfac,
    pr, pc, wr, wc, gf, cf, s, wp, r1, t, r2, u, r3, gp, grs, c0, c1, cy, cz, aug, ac,
    load_sem, send_sem, gsend, gdsend, gasend,
    pr_sem, pc_sem, wr_sem, wc_sem, r1_sem, r2_sem, r3_sem, grs_sem, gf_sem, cy_sem, cz_sem, cf_sem,
):
    p = lax.axis_index("row")
    q = lax.axis_index("col")
    zh, x, c = p // 8, (p // 2) % 4, p % 2
    zl, y = q // 4, q % 4
    same = p == q
    j = x * 2 + c

    load = pltpu.make_async_copy(s_hbm, s, load_sem)
    load.start()

    barrier = pltpu.get_barrier_semaphore()

    def hello(dev):
        pl.semaphore_signal(barrier, inc=1, device_id=dev, device_id_type=MESH)

    def greet(i, carry):
        hello((lax.rem(p + i, 16), q))
        hello((p, lax.rem(q + i, 16)))
        return carry

    lax.fori_loop(1, 16, greet, 0)
    pl.semaphore_wait(barrier, 30)
    load.wait()
    out = Sends(send_sem)

    def send_chunk(buf, sems, k, dev, cond=None):
        out.go(buf.at[chunk(k)], buf.at[chunk(k)], sems.at[k], dev, cond)

    def wait_chunk(buf, sems, k, cond=None):
        arrived(buf.at[chunk(k)], sems.at[k], cond)


    def col_of(i, n):
        return lax.rem(zl + i, 4) * 4 + lax.rem(y + n, 4)

    def col_z(buf, sems, root):
        for i in (1, 3, 2):
            d = col_of(i, 0)
            send_chunk(buf, sems, q, (p, d), (d != 0) if root else None)

    def col_y(buf, sems, root, i):
        k = col_of(i, 0)
        if i:
            wait_chunk(buf, sems, k, (q != 0) if root else None)
        for n in (1, 3, 2):
            d = col_of(0, n)
            send_chunk(buf, sems, k, (p, d), (d != 0) if root else None)

    def col_finish(buf, sems, root):
        for i in (0, 1, 3, 2):
            for n in (1, 3, 2):
                wait_chunk(buf, sems, col_of(i, n), (q != 0) if root else None)


    def pair_send(buf, sems, k, d, cond):
        view = buf.reshape(2, 8, CH, N)
        out.go(view.at[:, k], view.at[:, k], sems.at[k], (d, q), cond)

    def pair_wait(buf, sems, k, cond):
        arrived(buf.reshape(2, 8, CH, N).at[:, k], sems.at[k], cond)

    def pair_spread(buf, sems, here):
        for i in (1, 3, 2):
            d = zh * 8 + lax.rem(x + i, 4) * 2 + c
            pair_send(buf, sems, j, d, here & (d != 0))
        d = zh * 8 + x * 2 + 1 - c
        pair_send(buf, sems, j, d, here & (d != 0))

    def pair_forward(buf, sems, root):
        d = zh * 8 + x * 2 + 1 - c
        for i in (1, 3, 2):
            k = lax.rem(x + i, 4) * 2 + c
            pair_wait(buf, sems, k, (p != 0) if root else None)
            pair_send(buf, sems, k, d, (d != 0) if root else None)

    def pair_finish(buf, sems, root):
        for i in (0, 1, 3, 2):
            pair_wait(buf, sems, lax.rem(x + i, 4) * 2 + 1 - c, (p != 0) if root else None)


    def row_of(z, i, core):
        return z * 8 + lax.rem(x + i, 4) * 2 + core

    def row_spread(buf, sems, k):
        for i in (1, 3, 2):
            send_chunk(buf, sems, k, (row_of(zh, i, c), q))
        send_chunk(buf, sems, k, (row_of(zh, 0, 1 - c), q))

    def row_start(buf, sems):
        send_chunk(buf, sems, p, (row_of(1 - zh, 0, c), q))
        row_spread(buf, sems, p)

    def row_partner(buf, sems):
        k = row_of(1 - zh, 0, c)
        wait_chunk(buf, sems, k)
        row_spread(buf, sems, k)

    def row_own(buf, sems, z):
        for i in (1, 3, 2):
            k = row_of(z, i, c)
            wait_chunk(buf, sems, k)
            send_chunk(buf, sems, k, (row_of(zh, 0, 1 - c), q))

    def row_finish(buf, sems):
        for z in (zh, 1 - zh):
            for i in (0, 1, 3, 2):
                wait_chunk(buf, sems, row_of(z, i, 1 - c))


    def direct(src, dst, ssem, rsem, dev):
        return pltpu.make_async_remote_copy(
            src_ref=src, dst_ref=dst, send_sem=ssem, recv_sem=rsem, device_id=dev, device_id_type=MESH
        )

    def gram_copy(i):
        d = lax.rem(q + i, 16)
        return direct(gp.at[chunk(d)], grs.at[q], gsend.at[i], grs_sem.at[q], (p, d))

    def gram_all(i):
        d = lax.rem(q + i, 16)
        return direct(gf.at[chunk(q)], gf.at[chunk(q)], gasend.at[i], gf_sem.at[q], (p, d))

    def gram_down(i):
        return direct(gf.at[chunk(q)], gf.at[chunk(q)], gdsend.at[i], gf_sem.at[q], (i, q))

    def start_all(make):
        lax.fori_loop(1, 16, lambda i, z: (make(i).start(), z)[1], 0)

    def drain_all(make):
        lax.fori_loop(1, 16, lambda i, z: (make(i).wait_send(), z)[1], 0)

    def wait_slots(buf, sems, me):
        def step(i, z):
            k = lax.rem(me + i, 16)
            arrived(buf.at[k], sems.at[k])
            return z

        lax.fori_loop(1, 16, step, 0)

    def wait_chunks(buf, sems, me):
        def step(i, z):
            wait_chunk(buf, sems, lax.rem(me + i, 16))
            return z

        lax.fori_loop(1, 16, step, 0)

    lane = lax.broadcasted_iota(jnp.int32, (NB, N), 1)

    @pl.when(p == 0)
    def _():
        pc[...] = jnp.where((q == 0) & (lane < NB), 0.0, s[0:NB, :])

    for k in (4, 5, 2, 3, 6, 7, 1):
        pair_send(pc, pc_sem, k, k, p == 0)

    @pl.when(p == 0)
    def _():
        both = split(pc[...])
        gp[...] = dot3s(both, both, LAST)
        grs[pl.ds(q, 1)] = gp[chunk(q), :][None]
        start_all(gram_copy)

    @pl.when(q == 0)
    def _():
        pr[...] = jnp.where((p == 0) & (lane < NB), 0.0, s[:, 0:NB].T)

    for i in range(4):
        for n in (1, 3, 2):
            send_chunk(pr, pr_sem, i * 4 + n, (p, n), q == 0)

    def line(i, here):
        k = i * 4 + y
        wait_chunk(pr, pr_sem, k, here & (q != 0))
        send_chunk(pr, pr_sem, k, (p, lax.rem(q + 4, 16)), here & (zl < 3))
        for n in (1, 3, 2):
            d = col_of(0, n)
            send_chunk(pr, pr_sem, k, (p, d), here & (d != 0))

    near, far, first = zh == 0, zh == 1, zl == 0
    line(0, first)
    pair_wait(pc, pc_sem, j, near & (p != 0))
    pair_send(pc, pc_sem, j, 8 + j, near)
    pair_spread(pc, pc_sem, near)
    line(0, zl > 0)
    line(1, zl >= 0)

    @pl.when(p == 0)
    def _():
        wait_slots(grs, grs_sem, q)
        gf[chunk(q), :] = jnp.sum(grs[...], axis=0)
        start_all(gram_down)

    line(2, zl >= 0)
    pair_wait(pc, pc_sem, j, far)
    pair_spread(pc, pc_sem, far)
    line(3, zl >= 0)
    pair_forward(pc, pc_sem, True)
    pair_finish(pc, pc_sem, True)
    wait_chunk(gf, gf_sem, q, p != 0)
    start_all(gram_all)

    col_finish(pr, pr_sem, True)
    prh, prl = split(pr[...])

    def product(i, z):
        cols = pl.ds(pl.multiple_of(i * 256, 256), 256)
        wp.reshape(NB, N)[:, cols] = dot3s((prh, prl), split(s[:, cols]), PLAIN)
        return z

    for part in (0, 1):
        lax.fori_loop(2 * part, 2 * part + 2, product, 0)
        cols = pl.ds(part * 512, 512)
        out.go(
            wp.at[:, 1 - c, :, cols], r1.at[:, :, cols], r1_sem.at[part], (zh * 8 + x * 2 + 1 - c, q)
        )
    for part in (0, 1):
        arrived(r1.at[:, :, pl.ds(part * 512, 512)], r1_sem.at[part])
    t[...] = wp[:, pl.ds(c, 1)][:, 0] + r1[...]
    for phase, z in ((0, 1 - zh), (1, zh)):
        for i in (1, 3, 2):
            xx = lax.rem(x + i, 4)
            out.go(t.at[z * 4 + xx], r2.at[phase, i - 1], r2_sem.at[phase, i - 1], (zh * 8 + xx * 2 + c, q))
    wait_chunks(gf, gf_sem, q)
    row = lax.broadcasted_iota(jnp.int32, (NB, NB), 0)
    col = lax.broadcasted_iota(jnp.int32, (NB, NB), 1)
    aug[:, 0:NB] = gf[...]
    aug[:, NB:] = (row == col).astype(F32)
    factor_block(aug, 0)
    for i in (1, 3, 2):
        arrived(r2.at[0, i - 1], r2_sem.at[0, i - 1])
    u[...] = t[(1 - zh) * 4 + x] + (r2[0, 0] + r2[0, 1] + r2[0, 2])
    out.go(u, r3, r3_sem, ((1 - zh) * 8 + j, q))
    factor_block(aug, 1)
    for i in (1, 3, 2):
        arrived(r2.at[1, i - 1], r2_sem.at[1, i - 1])
    part = t[zh * 4 + x] + (r2[1, 0] + r2[1, 1] + r2[1, 2])
    arrived(r3, r3_sem)
    mine = part + r3[...]
    wc[chunk(p), :] = mine

    curv = cf.reshape(2, 4, 2, CH, NB)
    c0[...] = dot3(mine, pc[...], LAST)
    for i in (1, 3, 2):
        out.go(c0, cy.at[i - 1], cy_sem.at[i - 1], (p, col_of(0, i)))
    out.go(wc.at[chunk(p)], wr.at[chunk(p)], wr_sem.at[p], (q, p), p != q)
    row_start(wc, wc_sem)

    @pl.when(same)
    def _():
        wr[chunk(q), :] = mine

    factor_block(aug, 2)
    for i in (1, 3, 2):
        arrived(cy.at[i - 1], cy_sem.at[i - 1])
    c1[...] = c0[...] + (cy[0] + cy[1] + cy[2])
    for i in (1, 3, 2):
        out.go(c1, cz.at[i - 1], cz_sem.at[i - 1], (p, col_of(i, 0)))
    factor_block(aug, 3)
    wait_chunk(wr, wr_sem, q, p != q)
    col_z(wr, wr_sem, False)
    col_y(wr, wr_sem, False, 0)
    for i in (1, 3, 2):
        arrived(cz.at[i - 1], cz_sem.at[i - 1])
    cf[chunk(p), :] = c1[...] + (cz[0] + cz[1] + cz[2])
    out.go(cf.at[chunk(p)], cf.at[chunk(p)], cf_sem.at[0], (row_of(1 - zh, 0, c), q))
    row_partner(wc, wc_sem)
    rfac[...] = jnp.where(row <= col, aug[:, 0:NB], 0.0)
    inverse = aug[:, NB:]
    m = split(2.0 * dot6(inverse, inverse, FIRST))
    ac[...] = dot3s(m, split(pc[...]), PLAIN)
    ah, al = split(ac[...])
    right[NB : 2 * NB, :] = ah
    right[3 * NB : 4 * NB, :] = al
    for i in (1, 3, 2):
        col_y(wr, wr_sem, False, i)
    arrived(cf.at[chunk(row_of(1 - zh, 0, c))], cf_sem.at[0])
    for i in (1, 3, 2):
        out.go(curv.at[:, x, c], curv.at[:, x, c], cf_sem.at[i], (row_of(zh, i, c), q))
    row_own(wc, wc_sem, zh)
    rh, rl = split(dot3s(m, split(pr[...]), PLAIN).T)
    left[:, 0:NB] = rh
    left[:, 2 * NB : 3 * NB] = rl
    for i in (1, 3, 2):
        arrived(curv.at[:, lax.rem(x + 4 - i, 4), c], cf_sem.at[i])
    out.go(curv.at[:, :, c], curv.at[:, :, c], cf_sem.at[4], (row_of(zh, 0, 1 - c), q))
    row_own(wc, wc_sem, 1 - zh)
    arrived(curv.at[:, :, 1 - c], cf_sem.at[4])

    turned = dot3s(split(cf[...]), (ah, al), PLAIN)
    row_finish(wc, wc_sem)
    vh, vl = split(wc[...] - turned)
    right[0:NB, :] = vh
    right[2 * NB : 3 * NB, :] = vl
    col_finish(wr, wr_sem, False)
    vh, vl = split(wr[...].T)
    left[:, NB : 2 * NB] = vh
    left[:, 3 * NB : 4 * NB] = vl
    out.drain()

    @pl.when(p == 0)
    def _():
        drain_all(gram_copy)
        drain_all(gram_down)

    drain_all(gram_all)


def exchange(matrix):
    vm = pl.BlockSpec(memory_space=pltpu.VMEM)
    dma = pltpu.SemaphoreType.DMA
    big = pltpu.VMEM((NB, N), F32)
    small = pltpu.VMEM((NB, NB), F32)
    return pl.pallas_call(
        exchange_kernel,
        out_shape=(
            jax.ShapeDtypeStruct((N, 4 * NB), BF16),
            jax.ShapeDtypeStruct((4 * NB, N), BF16),
            jax.ShapeDtypeStruct((NB, NB), F32),
        ),
        in_specs=[pl.BlockSpec(memory_space=pltpu.HBM)],
        out_specs=(vm,) * 3,
        scratch_shapes=[
            big, big, big, big, small, small,
            pltpu.VMEM((N, N), F32),
            pltpu.VMEM((8, 2, CH, N), F32),
            pltpu.VMEM((8, CH, N), F32),
            pltpu.VMEM((8, CH, N), F32),
            pltpu.VMEM((2, 3, CH, N), F32),
            pltpu.VMEM((CH, N), F32),
            pltpu.VMEM((CH, N), F32),
            small,
            pltpu.VMEM((16, CH, NB), F32),
            pltpu.VMEM((CH, NB), F32),
            pltpu.VMEM((CH, NB), F32),
            pltpu.VMEM((3, CH, NB), F32),
            pltpu.VMEM((3, CH, NB), F32),
            pltpu.VMEM((NB, 2 * NB), F32),
            big,
            dma, dma((112,)), dma((16,)), dma((16,)), dma((16,)),
            dma((16,)), dma((8,)), dma((16,)), dma((16,)), dma((2,)), dma((2, 3)), dma,
            dma((16,)), dma((16,)), dma((3,)), dma((3,)), dma((5,)),
        ],
        compiler_params=pltpu.CompilerParams(collective_id=0, has_side_effects=True, vmem_limit_bytes=48 << 20),
        name="exchange",
    )(matrix)


TILE = 128


def finish_kernel(left, right, factor, s, out, r, buf, sems, r_sem):
    r_copy = pltpu.make_async_copy(factor, r, r_sem)
    r_copy.start()
    half = 2 * NB
    copies = []
    for i in range(N // TILE):
        rows = slice(i * TILE, (i + 1) * TILE)
        lh, ll = left[rows, 0:half], left[rows, half:]
        rh, rl = right[0:half, :], right[half:, :]
        buf[rows, :] = s[rows, :] - (dot(lh, rh, PLAIN) + (dot(lh, rl, PLAIN) + dot(ll, rh, PLAIN)))
        copies.append(pltpu.make_async_copy(buf.at[rows], out.at[rows], sems.at[i]))
        copies[-1].start()
    for copy in copies:
        copy.wait()
    r_copy.wait()


def finish(left, right, factor, matrix):
    vm, anywhere = pl.BlockSpec(memory_space=pltpu.VMEM), pl.BlockSpec(memory_space=pl.ANY)
    dma = pltpu.SemaphoreType.DMA
    return pl.pallas_call(
        finish_kernel,
        out_shape=(jax.ShapeDtypeStruct((N, N), F32), jax.ShapeDtypeStruct((NB, NB), F32)),
        in_specs=[vm] * 4,
        out_specs=(anywhere, anywhere),
        scratch_shapes=[pltpu.VMEM((N, N), F32), dma((N // TILE,)), dma],
        compiler_params=pltpu.CompilerParams(vmem_limit_bytes=32 << 20),
        name="finish",
    )(left, right, factor, matrix)


def on_device(matrix):
    return finish(*exchange(matrix), matrix)


def solution(mesh):
    return jax.shard_map(
        on_device,
        mesh=mesh,
        in_specs=(P("row", "col"),),
        out_specs=(P("row", "col"), P()),
        check_vma=False,
    )
```
